256 devices in a mesh: segment: 8 (over x, core), dp: 32 (over y, z).
Axes of the slice: x: 4, y: 4, z: 8, core: 2. Of those that a mesh axis runs over, the one named last changes fastest.
Arguments:
- histories: bfloat16 [512, 32, 2048], P('dp'), may hold values from -6 to 6
- segment_weight: bfloat16 [8, 2048, 2048], P('segment'), may hold values from -0.125 to 0.125
- segment_gain: float32 [8, 2048], P('segment'), may hold values from 0.25 to 1.75
- item_table: bfloat16 [32768, 256], P('dp'), may hold values from -6 to 6
- item_weight: bfloat16 [256, 2048], replicated, may hold values from -0.375 to 0.375
- query_scale: float32 [512], P('dp'), may hold values from 0.5 to 1
- cand_bias: float32 [512, 128], P('dp', 'segment'), may hold values from -1 to 262
- cand_owner: int32 [512, 128], P('dp', 'segment'), may hold values from 0 to 31, as said below
- cand_slot: int32 [512, 128], P('dp', 'segment'), may hold values from 0 to 1023
Outputs:
- query_loss: float32 [512], P('dp')
- table_grad: float32 [32768, 256], P('dp')
The draws below stay inside these ranges and needn't reach their ends.
Inputs may be any that keep to these rules, and one draw needn't show every extreme that they name: `cand_owner`: within one device's block (the 16 queries of one dp index and the 16 candidates of one segment index), at most 32 candidates name one shard; one shard, the same for all blocks, is named exactly 32 times in every block.
All inputs are finite; a program needn't handle non-finite values.
Results may differ from the reference program's by a relative error of at most 0.015.
Values may be sent and summed in bfloat16 or wider, within the bound.
No kernel may reach another device: no remote copies, remote signals or barrier semaphores. Data moves between devices by JAX's collectives and lax.ppermute only.
A program may use at most 128 MiB of HBM per device.

```python
import math
import jax
import jax.numpy as jnp
from jax import lax

D = 2048
E = 256
LAYERS = 8
LEN = 32
Q_DEV = 16
C = 128
C_DEV = 16
REQ_DEV = 256
CAP = 32
ITEMS_DEV = 1024
ITEMS = 32768
QUERIES = 512
N_SEGMENT = 8
N_DP = 32


def draw_query_scale(key, part):
    key = jax.random.fold_in(key, 5)
    picked = jnp.exp(jax.random.uniform(key, (QUERIES,), jnp.float32, math.log(0.5), math.log(1.0)))
    return picked.astype(jnp.float32)


def draw_cand_bias(key, part):
    key = jax.random.fold_in(key, 17)
    base_key, section_key, noise_key, lift_key = jax.random.split(key, 4)
    base = jax.random.uniform(base_key, (QUERIES, 1, 1), jnp.float32, 0.0, 3.0)
    ramp = 1.2 * jnp.arange(N_SEGMENT, dtype=jnp.float32).reshape(1, N_SEGMENT, 1) / max(N_SEGMENT - 1, 1)
    section = ramp + jax.random.uniform(section_key, (QUERIES, N_SEGMENT, 1), jnp.float32, 0.0, 1.0)
    noise = jnp.clip(jax.random.normal(noise_key, (QUERIES, N_SEGMENT, C_DEV), jnp.float32), -3.0, 3.0)
    lift = jax.random.uniform(lift_key, (QUERIES,), jnp.float32, 5.0, 8.0)
    bias = (base + section + 0.1 * noise).reshape(QUERIES, C)
    positive = base.reshape(QUERIES) + lift
    first = (jnp.arange(C) == 0)[None, :]
    bias = jnp.where(first, positive[:, None], bias)
    return bias.astype(jnp.float32)


def draw_cand_owner(key, part):
    key = jax.random.fold_in(key, 11)
    blocks = N_DP * N_SEGMENT
    hot_key, start_key, perm_key = jax.random.split(key, 3)
    hot_owner = jax.random.randint(hot_key, (), 0, N_DP)
    starts = jax.random.randint(start_key, (blocks, 1), 0, N_DP - 1)
    orders = jax.vmap(lambda sub_key: jax.random.permutation(sub_key, REQ_DEV))(jax.random.split(perm_key, blocks))
    spread = (hot_owner + 1 + (starts + orders - CAP) % (N_DP - 1)) % N_DP
    owners = jnp.where(orders < CAP, hot_owner, spread)
    owners = owners.reshape(N_DP, N_SEGMENT, Q_DEV, C_DEV).transpose(0, 2, 1, 3)
    return owners.reshape(QUERIES, C).astype(jnp.int32)


def set_ends(drawn, key, low, top_value):
    longest = drawn.shape.index(max(drawn.shape))
    spots = []
    for shift in (0, 1):
        where = [jax.random.randint(jax.random.fold_in(key, axis), (), 0, length) for axis, length in enumerate(drawn.shape)]
        where[longest] = (where[longest] + shift) % drawn.shape[longest]
        spots.append(tuple(where))
    return drawn.at[spots[0]].set(low).at[spots[1]].set(top_value)


def steps_of(own_key, shape, shards, least, largest):
    def one(axis_at, shards_of):
        heights = jax.random.uniform(jax.random.fold_in(jax.random.fold_in(own_key, 6), axis_at), (shards_of,), jnp.float32, least / len(shards), largest / len(shards))
        return jnp.repeat(jnp.exp(heights), shape[axis_at] // shards_of).reshape((-1,) + (1,) * (len(shape) - axis_at - 1))

    level = one(*shards[0])
    for cut in shards[1:]:
        level = level * one(*cut)
    return level


def normal_values(key, dims, scale, bound, shards=(), kind=jnp.bfloat16):
    drawn = scale * jax.random.normal(key, dims, jnp.float32)
    if shards:
        drawn = drawn * steps_of(key, dims, shards, -0.22, 0.18)
    return jnp.clip(drawn, -bound, bound).astype(kind)


def setup_inputs(seed: int = 0) -> dict:
    seeds = jax.random.split(jax.random.key(seed), 10)
    return {
        "histories": normal_values(seeds[0], (QUERIES, LEN, D), 1.0, 6.0, ((0, 32),)),
        "segment_weight": normal_values(seeds[1], (LAYERS, D, D), D ** -0.5, 0.125, ((0, 8),)),
        "segment_gain": jnp.clip(1.0 + 0.15 * jax.random.normal(seeds[2], (LAYERS, D), jnp.float32), 0.25, 1.75),
        "item_table": normal_values(seeds[3], (ITEMS, E), 1.0, 6.0, ((0, 32),)),
        "item_weight": normal_values(seeds[4], (E, D), E ** -0.5, 0.375),
        "query_scale": draw_query_scale(jax.random.fold_in(seeds[9], 71), 0),
        "cand_bias": draw_cand_bias(jax.random.fold_in(seeds[9], 71), 0),
        "cand_owner": draw_cand_owner(jax.random.fold_in(seeds[9], 71), 0),
        "cand_slot": set_ends(jax.random.randint(seeds[8], (QUERIES, C), 0, ITEMS_DEV), jax.random.fold_in(seeds[8], 1), 0, ITEMS_DEV - 1).astype(jnp.int32),
    }


EPSILON = 1e-05

def layer_apply(hidden, weight, gain):
    widened = hidden.astype(jnp.float32)
    normed = (widened * lax.rsqrt(lax.optimization_barrier(jnp.mean(widened * widened, axis=-1, keepdims=True)) + EPSILON) * gain).astype(jnp.bfloat16)
    projected = jnp.dot(normed, weight, preferred_element_type=jnp.float32)
    return (widened + jax.nn.silu(projected)).astype(jnp.bfloat16)

def silu_slope(value):
    logistic = jax.nn.sigmoid(value)
    return logistic * (1.0 + value * (1.0 - logistic))

def reference(histories, segment_weight, segment_gain, item_table, item_weight, query_scale, cand_bias, cand_owner, cand_slot):
    hidden = histories.reshape(-1, D)
    for layer_no in range(LAYERS):
        hidden = layer_apply(hidden, segment_weight[layer_no], segment_gain[layer_no])
    pooled = lax.optimization_barrier(jnp.mean(hidden.astype(jnp.float32).reshape(QUERIES, LEN, D), axis=1))
    query_vec = (pooled * lax.rsqrt(lax.optimization_barrier(jnp.mean(pooled * pooled, axis=-1, keepdims=True)) + EPSILON)).astype(jnp.bfloat16)
    row_ids = (cand_owner * ITEMS_DEV + cand_slot).reshape(-1).astype(jnp.int32)
    fetched = item_table[row_ids]
    item_pre = jnp.dot(fetched, item_weight, preferred_element_type=jnp.float32)
    item_vec = jax.nn.silu(item_pre).astype(jnp.bfloat16).reshape(QUERIES, C, D)
    scores = query_scale[:, None] * jnp.einsum('qd,qcd->qc', query_vec.astype(jnp.float32), item_vec.astype(jnp.float32)) / math.sqrt(D) + cand_bias
    highest = lax.optimization_barrier(jnp.max(scores, axis=1))
    lse = highest + jnp.log(lax.optimization_barrier(jnp.sum(jnp.exp(scores - highest[:, None]), axis=1)))
    query_loss = lse - scores[:, 0]
    score_grad = jnp.exp(scores - lse[:, None]) - (jnp.arange(C) == 0).astype(jnp.float32)[None, :]
    vec_grad = ((score_grad * query_scale[:, None] / math.sqrt(D))[:, :, None] * query_vec.astype(jnp.float32)[:, None, :]).astype(jnp.bfloat16)
    pre_grad = (vec_grad.reshape(-1, D).astype(jnp.float32) * silu_slope(item_pre)).astype(jnp.bfloat16)
    row_grad = lax.dot_general(pre_grad, item_weight, (((1,), (1,)), ((), ())), preferred_element_type=jnp.float32).astype(jnp.bfloat16)
    table_grad = jnp.zeros((ITEMS, E), jnp.float32).at[row_ids].add(row_grad.astype(jnp.float32))
    return (query_loss, table_grad)
```

```python
import functools
import math

import jax
import jax.numpy as jnp
from jax import lax
from jax.experimental import pallas as pl
from jax.experimental.pallas import tpu as pltpu
from jax.sharding import PartitionSpec as P

EPSILON = 1e-05
SEGMENT = "segment"
DP = "dp"
KERNEL_VMEM = 12 * 2**20
IN_VMEM = pl.BlockSpec(memory_space=pltpu.VMEM)
IN_SMEM = pl.BlockSpec(memory_space=pltpu.SMEM)
ANYWHERE = pl.BlockSpec(memory_space=pl.ANY)


def to_other_core(value):
    count = lax.axis_size(SEGMENT)
    return lax.ppermute(value, SEGMENT, [(i, i ^ 1) for i in range(count)])


def to_chip(value, steps):
    count = lax.axis_size(SEGMENT)
    return lax.ppermute(value, SEGMENT, [(i, (i + 2 * steps) % count) for i in range(count)])


def load_kernel(source, held, sem):
    copy = pltpu.make_async_copy(source, held, sem)
    copy.start()
    copy.wait()


def held_in_vmem(weight):
    return pl.pallas_call(
        load_kernel,
        out_shape=pltpu.VMEM(weight.shape, weight.dtype),
        in_specs=[ANYWHERE],
        out_specs=IN_VMEM,
        scratch_shapes=[pltpu.SemaphoreType.DMA],
        compiler_params=pltpu.CompilerParams(vmem_limit_bytes=KERNEL_VMEM),
        cost_estimate=pl.CostEstimate(flops=0, bytes_accessed=2 * weight.size * 2, transcendentals=0),
        name="load_weight",
    )(weight)


def layer_into(source, weight, gain, normed, target):
    widened = source[...].astype(jnp.float32)
    mean_square = jnp.mean(widened * widened, axis=-1, keepdims=True)
    normed[...] = (widened * lax.rsqrt(mean_square + EPSILON) * gain[...]).astype(jnp.bfloat16)
    width = target.shape[1]
    tile = 512
    for start in range(0, width, tile):
        columns = pl.ds(start, tile)
        projected = jnp.dot(normed[...], weight[:, columns], preferred_element_type=jnp.float32)
        gated = projected / (1.0 + jnp.exp(-projected))
        target[:, columns] = (source[:, columns].astype(jnp.float32) + gated).astype(jnp.bfloat16)


def stage_kernel(has_injected, has_incoming, gives_rows, gives_means, *refs):
    refs = list(refs)
    place = refs.pop(0)
    injected = refs.pop(0) if has_injected else None
    incoming = refs.pop(0) if has_incoming else None
    own_weight, other_weight, own_gain, other_gain = refs[:4]
    refs = refs[4:]
    rows_out = refs.pop(0) if gives_rows else None
    means_out = refs.pop(0) if gives_means else None
    start, middle, normed, final = refs
    if rows_out is None:
        rows_out = final
    is_first, core = place[0], place[1]
    if has_injected and has_incoming:

        @pl.when(is_first == 1)
        def _():
            start[...] = injected[...]

        @pl.when(is_first == 0)
        def _():
            start[...] = incoming[...]

        begin = start
    else:
        begin = injected if has_injected else incoming

    @pl.when(core == 0)
    def _():
        layer_into(begin, own_weight, own_gain, normed, middle)
        layer_into(middle, other_weight, other_gain, normed, rows_out)

    @pl.when(core == 1)
    def _():
        layer_into(begin, other_weight, other_gain, normed, middle)
        layer_into(middle, own_weight, own_gain, normed, rows_out)

    if gives_means:
        groups = means_out.shape[0]
        length = rows_out.shape[0] // groups
        for k in range(groups):
            tokens = rows_out[pl.ds(k * length, length), :].astype(jnp.float32)
            means_out[pl.ds(k, 1), :] = jnp.mean(tokens, axis=0, keepdims=True)


def stage(place, injected, incoming, weights, gains, groups, gives_rows, gives_means):
    shape = (injected if injected is not None else incoming).shape
    rows, width = shape
    operands = [place]
    operands += [value for value in (injected, incoming) if value is not None]
    operands += [*weights, *gains]
    out_shape = []
    if gives_rows:
        out_shape.append(jax.ShapeDtypeStruct(shape, jnp.bfloat16))
    if gives_means:
        out_shape.append(jax.ShapeDtypeStruct((groups, width), jnp.float32))
    results = pl.pallas_call(
        functools.partial(
            stage_kernel, injected is not None, incoming is not None, gives_rows, gives_means
        ),
        out_shape=out_shape,
        in_specs=[IN_SMEM] + [IN_VMEM] * (len(operands) - 1),
        out_specs=[IN_VMEM] * len(out_shape),
        scratch_shapes=[pltpu.VMEM(shape, jnp.bfloat16)] * 4,
        compiler_params=pltpu.CompilerParams(vmem_limit_bytes=KERNEL_VMEM),
        cost_estimate=pl.CostEstimate(
            flops=4 * rows * width * width, bytes_accessed=4 * width * width, transcendentals=2 * rows * width
        ),
        name="stage",
    )(*operands)
    rows_out = results[0] if gives_rows else None
    means_out = results[-1] if gives_means else None
    return rows_out, means_out


def query_tower(histories, weight, gain, chip, core):
    query_count, seq_len, width = histories.shape
    chips = lax.axis_size(SEGMENT) // 2
    lane = query_count // 2
    group = 2
    groups = lane // group
    other_weight = to_other_core(weight)
    other_gain = to_other_core(gain)
    weights = (held_in_vmem(weight), held_in_vmem(other_weight))
    gains = (gain, other_gain)
    place = jnp.stack([(chip == 0).astype(jnp.int32), core.astype(jnp.int32)])
    gap = 2
    arriving = {}
    means = []
    for tick in range(groups + gap * (chips - 1)):
        injected = None
        if tick < groups:
            injected = lax.dynamic_slice_in_dim(
                histories, core * lane + tick * group, group, 0
            ).reshape(group * seq_len, width)
        incoming = arriving.pop(tick, None)
        busy = [c for c in range(chips) if 0 <= tick - gap * c < groups]
        sends = any(c < chips - 1 for c in busy)
        ends = chips - 1 in busy
        rows, mean = stage(place, injected, incoming, weights, gains, group, sends, ends)
        if sends:
            arriving[tick + gap] = to_chip(rows, 1)
        if ends:
            means.append(mean)
    return jnp.concatenate(means, axis=0)


def from_last_chip(value, chip):
    ahead, back, across = to_chip(value, 1), to_chip(value, -1), to_chip(value, 2)
    return jnp.where(
        chip == 3, value, jnp.where(chip == 0, ahead, jnp.where(chip == 2, back, across))
    )


def summed_over_segment(local, chip, core):
    rows, width = local.shape
    half, piece = rows // 2, rows // 8
    kept = lax.dynamic_slice_in_dim(local, core * half, half, 0)
    given = lax.dynamic_slice_in_dim(local, (1 - core) * half, half, 0).astype(jnp.bfloat16)
    part = kept + to_other_core(given).astype(jnp.float32)
    rounded = part.astype(jnp.bfloat16)

    def piece_of(array, index):
        return lax.dynamic_slice_in_dim(array, (index % 4) * piece, piece, 0)

    got = [to_chip(piece_of(rounded, chip + steps), steps) for steps in (1, 2, 3)]
    total = piece_of(part, chip)
    for term in got:
        total = total + term.astype(jnp.float32)
    total = total.astype(jnp.bfloat16)
    whole = jnp.zeros((half, width), jnp.bfloat16)
    for steps, term in enumerate([total] + [to_chip(total, steps) for steps in (1, 2, 3)]):
        whole = lax.dynamic_update_slice_in_dim(whole, term, ((chip - steps) % 4) * piece, 0)
    other = to_other_core(whole)
    low = jnp.where(core == 0, whole, other)
    high = jnp.where(core == 0, other, whole)
    return jnp.concatenate([low, high], axis=0)


def combine(earlier, later):
    highest = jnp.maximum(earlier[0], later[0])
    summed = earlier[1] * jnp.exp(earlier[0] - highest) + later[1] * jnp.exp(later[0] - highest)
    return jnp.stack([highest, summed, earlier[2] + later[2]])


def combined_over_segment(stats):
    stats = combine(stats, to_other_core(stats))
    ahead, back, across = to_chip(stats, 1), to_chip(stats, -1), to_chip(stats, 2)
    return combine(combine(stats, across), combine(ahead, back))


def shards(
    histories,
    segment_weight,
    segment_gain,
    item_table,
    item_weight,
    query_scale,
    cand_bias,
    cand_owner,
    cand_slot,
):
    segment_idx = lax.axis_index(SEGMENT)
    chip, core = segment_idx // 2, segment_idx % 2
    shard_count = lax.axis_size(DP)
    query_count, _, model_width = histories.shape
    cand_count = cand_owner.shape[1]
    count_rows = query_count * cand_count
    capacity = 4 * count_rows // shard_count
    slots = shard_count * capacity
    item_rows = item_table.shape[0]

    owner_ids = cand_owner.reshape(-1)
    slot_ids = cand_slot.reshape(-1)
    one_hot = owner_ids[:, None] == jnp.arange(shard_count, dtype=jnp.int32)[None, :]
    before = jnp.arange(count_rows)[:, None] > jnp.arange(count_rows)[None, :]
    ranks = jnp.dot(
        before.astype(jnp.bfloat16), one_hot.astype(jnp.bfloat16), preferred_element_type=jnp.float32
    )
    within = jnp.sum(jnp.where(one_hot, ranks, 0.0), axis=1).astype(jnp.int32)
    position = owner_ids * capacity + within
    placed = position[:, None] == jnp.arange(slots, dtype=jnp.int32)[None, :]
    outbox = jnp.sum(jnp.where(placed, slot_ids[:, None] + 1, 0), axis=0)
    placed = placed.astype(jnp.bfloat16)
    inbox = lax.all_to_all(
        outbox.reshape(shard_count, capacity), DP, split_axis=0, concat_axis=0, tiled=True
    ).reshape(-1)
    wanted = (inbox[:, None] - 1 == jnp.arange(item_rows, dtype=jnp.int32)[None, :]).astype(
        jnp.bfloat16
    )
    fetched = jnp.dot(wanted, item_table, preferred_element_type=jnp.float32).astype(jnp.bfloat16)
    returned = lax.all_to_all(
        fetched.reshape(shard_count, capacity, -1), DP, split_axis=0, concat_axis=0, tiled=True
    ).reshape(slots, -1)
    own_rows = jnp.dot(placed, returned, preferred_element_type=jnp.float32).astype(jnp.bfloat16)
    item_pre = jnp.dot(own_rows, item_weight, preferred_element_type=jnp.float32)
    logistic = jax.nn.sigmoid(item_pre)
    item_vec = (item_pre * logistic).astype(jnp.bfloat16)
    slope = logistic * (1.0 + item_pre * (1.0 - logistic))

    pooled = query_tower(histories, segment_weight[0], segment_gain, chip, core)
    lane_vec = (
        pooled * lax.rsqrt(jnp.mean(pooled * pooled, axis=-1, keepdims=True) + EPSILON)
    ).astype(jnp.bfloat16)
    lane_vec = from_last_chip(lane_vec, chip)
    other_vec = to_other_core(lane_vec)
    query_vec = jnp.concatenate(
        [jnp.where(core == 0, lane_vec, other_vec), jnp.where(core == 0, other_vec, lane_vec)],
        axis=0,
    )

    row_query = jnp.arange(count_rows, dtype=jnp.int32) // cand_count
    mine = row_query[:, None] == jnp.arange(query_count, dtype=jnp.int32)[None, :]
    products = lax.dot_general(
        item_vec, query_vec, (((1,), (1,)), ((), ())), preferred_element_type=jnp.float32
    )
    factor = query_scale[None, :] / math.sqrt(model_width)
    scores = query_scale[None, :] * products / math.sqrt(model_width) + cand_bias.reshape(-1)[:, None]
    highest = jnp.max(jnp.where(mine, scores, -jnp.inf), axis=0)
    shifted = jnp.exp(jnp.where(mine, scores - highest[None, :], -jnp.inf))
    summed = jnp.sum(shifted, axis=0)
    is_target = (jnp.arange(count_rows) % cand_count == 0)[:, None] & mine & (segment_idx == 0)
    positive = jnp.sum(jnp.where(is_target, scores, 0.0), axis=0)
    top, total, positive = combined_over_segment(jnp.stack([highest, summed, positive]))
    lse = top + jnp.log(total)
    query_loss = lse - positive

    widened = jnp.broadcast_to(
        query_vec.astype(jnp.float32)[:, None, :], (query_count, cand_count, model_width)
    ).reshape(count_rows, model_width)
    sloped = (widened * slope).astype(jnp.bfloat16)
    unscaled = lax.dot_general(
        sloped, item_weight, (((1,), (1,)), ((), ())), preferred_element_type=jnp.float32
    )
    score_grad = jnp.exp(jnp.where(mine, scores - lse[None, :], -jnp.inf)) - is_target
    row_factor = jnp.sum(score_grad * factor, axis=1)
    row_grad = (unscaled * row_factor[:, None]).astype(jnp.bfloat16)
    grad_box = lax.dot_general(
        placed, row_grad, (((0,), (0,)), ((), ())), preferred_element_type=jnp.float32
    ).astype(jnp.bfloat16)
    got_grad = lax.all_to_all(
        grad_box.reshape(shard_count, capacity, -1), DP, split_axis=0, concat_axis=0, tiled=True
    ).reshape(slots, -1)
    local_grad = lax.dot_general(
        wanted, got_grad, (((0,), (0,)), ((), ())), preferred_element_type=jnp.float32
    )
    table_grad = summed_over_segment(local_grad, chip, core).astype(jnp.float32)
    return (query_loss, table_grad)


def solution(mesh):
    return jax.shard_map(
        shards,
        mesh=mesh,
        in_specs=(
            P(DP, None, None),
            P(SEGMENT, None, None),
            P(SEGMENT, None),
            P(DP, None),
            P(),
            P(DP),
            P(DP, SEGMENT),
            P(DP, SEGMENT),
            P(DP, SEGMENT),
        ),
        out_specs=(P(DP), P(DP, None)),
        check_vma=False,
    )
```

```python
import functools
import math

import jax
import jax.numpy as jnp
from jax import lax
from jax.experimental import pallas as pl
from jax.experimental.pallas import tpu as pltpu
from jax.sharding import PartitionSpec as P

EPSILON = 1e-05
SEGMENT = "segment"
DP = "dp"
GROUP = 2
KERNEL_VMEM = 12 * 2**20
IN_VMEM = pl.BlockSpec(memory_space=pltpu.VMEM)
IN_SMEM = pl.BlockSpec(memory_space=pltpu.SMEM)
ANYWHERE = pl.BlockSpec(memory_space=pl.ANY)


def to_other_core(value):
    count = lax.axis_size(SEGMENT)
    return lax.ppermute(value, SEGMENT, [(i, i ^ 1) for i in range(count)])


def to_chip(value, steps):
    count = lax.axis_size(SEGMENT)
    return lax.ppermute(value, SEGMENT, [(i, (i + 2 * steps) % count) for i in range(count)])


def load_kernel(source, held, sem):
    copy = pltpu.make_async_copy(source, held, sem)
    copy.start()
    copy.wait()


def held_in_vmem(weight):
    return pl.pallas_call(
        load_kernel,
        out_shape=pltpu.VMEM(weight.shape, weight.dtype),
        in_specs=[ANYWHERE],
        out_specs=IN_VMEM,
        scratch_shapes=[pltpu.SemaphoreType.DMA],
        compiler_params=pltpu.CompilerParams(vmem_limit_bytes=KERNEL_VMEM),
        cost_estimate=pl.CostEstimate(flops=0, bytes_accessed=2 * weight.size * 2, transcendentals=0),
        name="load_weight",
    )(weight)


def layer_into(source, weight, gain, normed, target):
    widened = source[...].astype(jnp.float32)
    mean_square = jnp.mean(widened * widened, axis=-1, keepdims=True)
    normed[...] = (widened * lax.rsqrt(mean_square + EPSILON) * gain[...]).astype(jnp.bfloat16)
    width = target.shape[1]
    tile = 512
    for start in range(0, width, tile):
        columns = pl.ds(start, tile)
        projected = jnp.dot(normed[...], weight[:, columns], preferred_element_type=jnp.float32)
        gated = projected / (1.0 + jnp.exp(-projected))
        target[:, columns] = (source[:, columns].astype(jnp.float32) + gated).astype(jnp.bfloat16)


def stage_kernel(has_injected, has_incoming, gives_rows, gives_means, *refs):
    refs = list(refs)
    place = refs.pop(0)
    injected = refs.pop(0) if has_injected else None
    incoming = refs.pop(0) if has_incoming else None
    own_weight, other_weight, own_gain, other_gain = refs[:4]
    refs = refs[4:]
    rows_out = refs.pop(0) if gives_rows else None
    means_out = refs.pop(0) if gives_means else None
    start, middle, normed, final = refs
    if rows_out is None:
        rows_out = final
    is_first, core = place[0], place[1]
    if has_injected and has_incoming:

        @pl.when(is_first == 1)
        def _():
            start[...] = injected[...]

        @pl.when(is_first == 0)
        def _():
            start[...] = incoming[...]

        begin = start
    else:
        begin = injected if has_injected else incoming

    @pl.when(core == 0)
    def _():
        layer_into(begin, own_weight, own_gain, normed, middle)
        layer_into(middle, other_weight, other_gain, normed, rows_out)

    @pl.when(core == 1)
    def _():
        layer_into(begin, other_weight, other_gain, normed, middle)
        layer_into(middle, own_weight, own_gain, normed, rows_out)

    if gives_means:
        groups = means_out.shape[0]
        length = rows_out.shape[0] // groups
        for k in range(groups):
            tokens = rows_out[pl.ds(k * length, length), :].astype(jnp.float32)
            means_out[pl.ds(k, 1), :] = jnp.mean(tokens, axis=0, keepdims=True)


def stage(place, injected, incoming, weights, gains, groups, gives_rows, gives_means):
    shape = (injected if injected is not None else incoming).shape
    rows, width = shape
    operands = [place]
    operands += [value for value in (injected, incoming) if value is not None]
    operands += [*weights, *gains]
    out_shape = []
    if gives_rows:
        out_shape.append(jax.ShapeDtypeStruct(shape, jnp.bfloat16))
    if gives_means:
        out_shape.append(jax.ShapeDtypeStruct((groups, width), jnp.float32))
    results = pl.pallas_call(
        functools.partial(
            stage_kernel, injected is not None, incoming is not None, gives_rows, gives_means
        ),
        out_shape=out_shape,
        in_specs=[IN_SMEM] + [IN_VMEM] * (len(operands) - 1),
        out_specs=[IN_VMEM] * len(out_shape),
        scratch_shapes=[pltpu.VMEM(shape, jnp.bfloat16)] * 4,
        compiler_params=pltpu.CompilerParams(vmem_limit_bytes=KERNEL_VMEM),
        cost_estimate=pl.CostEstimate(
            flops=4 * rows * width * width, bytes_accessed=4 * rows * width, transcendentals=2 * rows * width
        ),
        name="stage",
    )(*operands)
    rows_out = results[0] if gives_rows else None
    means_out = results[-1] if gives_means else None
    return rows_out, means_out


def lane_groups(histories, core):
    query_count, seq_len, width = histories.shape
    lane = query_count // 2
    mine = lax.dynamic_slice_in_dim(histories, core * lane, lane, 0)
    return [
        mine[first : first + GROUP].reshape(GROUP * seq_len, width)
        for first in range(0, lane, GROUP)
    ]


def query_tower(place, injected, weight, other_weight, gain, other_gain):
    chips = lax.axis_size(SEGMENT) // 2
    groups = len(injected)
    weights = (held_in_vmem(weight), held_in_vmem(other_weight))
    gains = (gain, other_gain)
    gap = 2
    arriving = {}
    means = []
    for tick in range(groups + gap * (chips - 1)):
        begun = injected[tick] if tick < groups else None
        incoming = arriving.pop(tick, None)
        busy = [c for c in range(chips) if 0 <= tick - gap * c < groups]
        sends = any(c < chips - 1 for c in busy)
        ends = chips - 1 in busy
        rows, mean = stage(place, begun, incoming, weights, gains, GROUP, sends, ends)
        if sends:
            arriving[tick + gap] = to_chip(rows, 1)
        if ends:
            means.append(mean)
    return jnp.concatenate(means, axis=0)


def from_last_chip(value, chip):
    ahead, back, across = to_chip(value, 1), to_chip(value, -1), to_chip(value, 2)
    return jnp.where(
        chip == 3, value, jnp.where(chip == 0, ahead, jnp.where(chip == 2, back, across))
    )


def summed_over_segment(local, chip, core):
    rows, width = local.shape
    half, piece = rows // 2, rows // 8
    kept = lax.dynamic_slice_in_dim(local, core * half, half, 0)
    given = lax.dynamic_slice_in_dim(local, (1 - core) * half, half, 0).astype(jnp.bfloat16)
    part = kept + to_other_core(given).astype(jnp.float32)
    rounded = part.astype(jnp.bfloat16)

    def piece_of(array, index):
        return lax.dynamic_slice_in_dim(array, (index % 4) * piece, piece, 0)

    got = [to_chip(piece_of(rounded, chip + steps), steps) for steps in (1, 2, 3)]
    total = piece_of(part, chip)
    for term in got:
        total = total + term.astype(jnp.float32)
    total = total.astype(jnp.bfloat16)
    whole = jnp.zeros((half, width), jnp.bfloat16)
    for steps, term in enumerate([total] + [to_chip(total, steps) for steps in (1, 2, 3)]):
        whole = lax.dynamic_update_slice_in_dim(whole, term, ((chip - steps) % 4) * piece, 0)
    other = to_other_core(whole)
    low = jnp.where(core == 0, whole, other)
    high = jnp.where(core == 0, other, whole)
    return jnp.concatenate([low, high], axis=0)


def combine(earlier, later):
    highest = jnp.maximum(earlier[0], later[0])
    summed = earlier[1] * jnp.exp(earlier[0] - highest) + later[1] * jnp.exp(later[0] - highest)
    return jnp.stack([highest, summed, earlier[2] + later[2]])


def combined_over_segment(stats):
    stats = combine(stats, to_other_core(stats))
    ahead, back, across = to_chip(stats, 1), to_chip(stats, -1), to_chip(stats, 2)
    return combine(combine(stats, across), combine(ahead, back))


def shards(
    histories,
    segment_weight,
    segment_gain,
    item_table,
    item_weight,
    query_scale,
    cand_bias,
    cand_owner,
    cand_slot,
):
    segment_idx = lax.axis_index(SEGMENT)
    chip, core = segment_idx // 2, segment_idx % 2
    shard_count = lax.axis_size(DP)
    query_count, _, model_width = histories.shape
    cand_count = cand_owner.shape[1]
    count_rows = query_count * cand_count
    capacity = 4 * count_rows // shard_count
    slots = shard_count * capacity
    item_rows = item_table.shape[0]

    owner_ids = cand_owner.reshape(-1)
    slot_ids = cand_slot.reshape(-1)
    one_hot = owner_ids[:, None] == jnp.arange(shard_count, dtype=jnp.int32)[None, :]
    before = jnp.arange(count_rows)[:, None] > jnp.arange(count_rows)[None, :]
    ranks = jnp.dot(
        before.astype(jnp.bfloat16), one_hot.astype(jnp.bfloat16), preferred_element_type=jnp.float32
    )
    within = jnp.sum(jnp.where(one_hot, ranks, 0.0), axis=1).astype(jnp.int32)
    position = owner_ids * capacity + within
    placed = position[:, None] == jnp.arange(slots, dtype=jnp.int32)[None, :]
    outbox = jnp.sum(jnp.where(placed, slot_ids[:, None] + 1, 0), axis=0)
    placed = placed.astype(jnp.bfloat16)
    inbox = lax.all_to_all(
        outbox.reshape(shard_count, capacity), DP, split_axis=0, concat_axis=0, tiled=True
    ).reshape(-1)
    wanted = (inbox[:, None] - 1 == jnp.arange(item_rows, dtype=jnp.int32)[None, :]).astype(
        jnp.bfloat16
    )
    fetched = jnp.dot(wanted, item_table, preferred_element_type=jnp.float32).astype(jnp.bfloat16)
    weight = segment_weight[0]
    other_weight = to_other_core(weight)
    weight, other_weight, histories, fetched, placed, wanted = lax.optimization_barrier(
        (weight, other_weight, histories, fetched, placed, wanted)
    )
    returned = lax.all_to_all(
        fetched.reshape(shard_count, capacity, -1), DP, split_axis=0, concat_axis=0, tiled=True
    )
    place = jnp.stack([(chip == 0).astype(jnp.int32), core.astype(jnp.int32)])
    injected = lane_groups(histories, core)
    other_gain = to_other_core(segment_gain)
    pooled = lax.cond(
        cand_owner[0, 0] >= 0,
        query_tower,
        lambda *_: jnp.zeros((query_count // 2, model_width), jnp.float32),
        place,
        injected,
        weight,
        other_weight,
        segment_gain,
        other_gain,
    )
    returned, pooled = lax.optimization_barrier((returned, pooled))
    returned = returned.reshape(slots, -1)
    own_rows = jnp.dot(placed, returned, preferred_element_type=jnp.float32).astype(jnp.bfloat16)
    item_pre = jnp.dot(own_rows, item_weight, preferred_element_type=jnp.float32)
    logistic = jax.nn.sigmoid(item_pre)
    item_vec = (item_pre * logistic).astype(jnp.bfloat16)
    slope = logistic * (1.0 + item_pre * (1.0 - logistic))

    lane_vec = (
        pooled * lax.rsqrt(jnp.mean(pooled * pooled, axis=-1, keepdims=True) + EPSILON)
    ).astype(jnp.bfloat16)
    lane_vec = from_last_chip(lane_vec, chip)
    other_vec = to_other_core(lane_vec)
    query_vec = jnp.concatenate(
        [jnp.where(core == 0, lane_vec, other_vec), jnp.where(core == 0, other_vec, lane_vec)],
        axis=0,
    )

    row_query = jnp.arange(count_rows, dtype=jnp.int32) // cand_count
    mine = row_query[:, None] == jnp.arange(query_count, dtype=jnp.int32)[None, :]
    products = lax.dot_general(
        item_vec, query_vec, (((1,), (1,)), ((), ())), preferred_element_type=jnp.float32
    )
    factor = query_scale[None, :] / math.sqrt(model_width)
    scores = query_scale[None, :] * products / math.sqrt(model_width) + cand_bias.reshape(-1)[:, None]
    highest = jnp.max(jnp.where(mine, scores, -jnp.inf), axis=0)
    shifted = jnp.exp(jnp.where(mine, scores - highest[None, :], -jnp.inf))
    summed = jnp.sum(shifted, axis=0)
    is_target = (jnp.arange(count_rows) % cand_count == 0)[:, None] & mine & (segment_idx == 0)
    positive = jnp.sum(jnp.where(is_target, scores, 0.0), axis=0)
    top, total, positive = combined_over_segment(jnp.stack([highest, summed, positive]))
    lse = top + jnp.log(total)
    query_loss = lse - positive

    widened = jnp.broadcast_to(
        query_vec.astype(jnp.float32)[:, None, :], (query_count, cand_count, model_width)
    ).reshape(count_rows, model_width)
    sloped = (widened * slope).astype(jnp.bfloat16)
    unscaled = lax.dot_general(
        sloped, item_weight, (((1,), (1,)), ((), ())), preferred_element_type=jnp.float32
    )
    score_grad = jnp.exp(jnp.where(mine, scores - lse[None, :], -jnp.inf)) - is_target
    row_factor = jnp.sum(score_grad * factor, axis=1)
    row_grad = (unscaled * row_factor[:, None]).astype(jnp.bfloat16)
    grad_box = lax.dot_general(
        placed, row_grad, (((0,), (0,)), ((), ())), preferred_element_type=jnp.float32
    ).astype(jnp.bfloat16)
    got_grad = lax.all_to_all(
        grad_box.reshape(shard_count, capacity, -1), DP, split_axis=0, concat_axis=0, tiled=True
    ).reshape(slots, -1)
    local_grad = lax.dot_general(
        wanted, got_grad, (((0,), (0,)), ((), ())), preferred_element_type=jnp.float32
    )
    table_grad = summed_over_segment(local_grad, chip, core).astype(jnp.float32)
    return (query_loss, table_grad)


def solution(mesh):
    return jax.shard_map(
        shards,
        mesh=mesh,
        in_specs=(
            P(DP, None, None),
            P(SEGMENT, None, None),
            P(SEGMENT, None),
            P(DP, None),
            P(),
            P(DP),
            P(DP, SEGMENT),
            P(DP, SEGMENT),
            P(DP, SEGMENT),
        ),
        out_specs=(P(DP), P(DP, None)),
        check_vma=False,
    )
```

```python
import functools
import math

import jax
import jax.numpy as jnp
from jax import lax
from jax.experimental import pallas as pl
from jax.experimental.pallas import tpu as pltpu
from jax.sharding import PartitionSpec as P

EPSILON = 1e-05
SEGMENT = "segment"
DP = "dp"
GROUP = 2
TILE = 512
KERNEL_VMEM = 12 * 2**20
IN_VMEM = pl.BlockSpec(memory_space=pltpu.VMEM)
IN_SMEM = pl.BlockSpec(memory_space=pltpu.SMEM)
ANYWHERE = pl.BlockSpec(memory_space=pl.ANY)


def to_other_core(value):
    count = lax.axis_size(SEGMENT)
    return lax.ppermute(value, SEGMENT, [(i, i ^ 1) for i in range(count)])


def to_chip(value, steps):
    count = lax.axis_size(SEGMENT)
    return lax.ppermute(value, SEGMENT, [(i, (i + 2 * steps) % count) for i in range(count)])


def column_tiles(width):
    return [pl.ds(start, TILE) for start in range(0, width, TILE)]


def layer_into(source, weight, gain, normed, target, arrivals=None):
    widened = source[...].astype(jnp.float32)
    mean_square = jnp.mean(widened * widened, axis=-1, keepdims=True)
    normed[...] = (widened * lax.rsqrt(mean_square + EPSILON) * gain[...]).astype(jnp.bfloat16)
    for k, columns in enumerate(column_tiles(target.shape[1])):
        if arrivals is not None:
            arrivals[k].wait()
        projected = jnp.dot(normed[...], weight[:, columns], preferred_element_type=jnp.float32)
        gated = projected / (1.0 + jnp.exp(-projected))
        target[:, columns] = (source[:, columns].astype(jnp.float32) + gated).astype(jnp.bfloat16)


def first_stage_kernel(
    place, injected, own_source, other_source, own_gain, other_gain,
    rows_out, own_weight, other_weight, middle, normed, sems,
):
    def arriving(source, held, first):
        return [
            pltpu.make_async_copy(source.at[:, columns], held.at[:, columns], sems.at[first + k])
            for k, columns in enumerate(column_tiles(held.shape[1]))
        ]

    own = arriving(own_source, own_weight, 0)
    other = arriving(other_source, other_weight, len(own))

    def layers(first, first_weight, first_gain, second, second_weight, second_gain):
        for copy in first + second:
            copy.start()
        layer_into(injected, first_weight, first_gain, normed, middle, first)
        layer_into(middle, second_weight, second_gain, normed, rows_out, second)

    @pl.when(place[1] == 0)
    def _():
        layers(own, own_weight, own_gain, other, other_weight, other_gain)

    @pl.when(place[1] == 1)
    def _():
        layers(other, other_weight, other_gain, own, own_weight, own_gain)


def first_stage(place, injected, weight, other_weight, gains):
    rows, width = injected.shape
    copies = 2 * len(column_tiles(width))
    return pl.pallas_call(
        first_stage_kernel,
        out_shape=[
            jax.ShapeDtypeStruct(injected.shape, jnp.bfloat16),
            pltpu.VMEM(weight.shape, weight.dtype),
            pltpu.VMEM(weight.shape, weight.dtype),
        ],
        in_specs=[IN_SMEM, IN_VMEM, ANYWHERE, ANYWHERE, IN_VMEM, IN_VMEM],
        out_specs=[IN_VMEM] * 3,
        scratch_shapes=[pltpu.VMEM(injected.shape, jnp.bfloat16)] * 2
        + [pltpu.SemaphoreType.DMA((copies,))],
        compiler_params=pltpu.CompilerParams(vmem_limit_bytes=KERNEL_VMEM),
        cost_estimate=pl.CostEstimate(
            flops=4 * rows * width * width,
            bytes_accessed=4 * width * width,
            transcendentals=2 * rows * width,
        ),
        name="first_stage",
    )(place, injected, weight, other_weight, *gains)


def stage_kernel(has_injected, has_incoming, gives_rows, gives_means, *refs):
    refs = list(refs)
    place = refs.pop(0)
    injected = refs.pop(0) if has_injected else None
    incoming = refs.pop(0) if has_incoming else None
    own_weight, other_weight, own_gain, other_gain = refs[:4]
    refs = refs[4:]
    rows_out = refs.pop(0) if gives_rows else None
    means_out = refs.pop(0) if gives_means else None
    start, middle, normed, final = refs
    if rows_out is None:
        rows_out = final
    is_first, core = place[0], place[1]
    if has_injected and has_incoming:

        @pl.when(is_first == 1)
        def _():
            start[...] = injected[...]

        @pl.when(is_first == 0)
        def _():
            start[...] = incoming[...]

        begin = start
    else:
        begin = injected if has_injected else incoming

    @pl.when(core == 0)
    def _():
        layer_into(begin, own_weight, own_gain, normed, middle)
        layer_into(middle, other_weight, other_gain, normed, rows_out)

    @pl.when(core == 1)
    def _():
        layer_into(begin, other_weight, other_gain, normed, middle)
        layer_into(middle, own_weight, own_gain, normed, rows_out)

    if gives_means:
        groups = means_out.shape[0]
        length = rows_out.shape[0] // groups
        for k in range(groups):
            tokens = rows_out[pl.ds(k * length, length), :].astype(jnp.float32)
            means_out[pl.ds(k, 1), :] = jnp.mean(tokens, axis=0, keepdims=True)


def stage(place, injected, incoming, weights, gains, groups, gives_rows, gives_means):
    shape = (injected if injected is not None else incoming).shape
    rows, width = shape
    operands = [place]
    operands += [value for value in (injected, incoming) if value is not None]
    operands += [*weights, *gains]
    out_shape = []
    if gives_rows:
        out_shape.append(jax.ShapeDtypeStruct(shape, jnp.bfloat16))
    if gives_means:
        out_shape.append(jax.ShapeDtypeStruct((groups, width), jnp.float32))
    results = pl.pallas_call(
        functools.partial(
            stage_kernel, injected is not None, incoming is not None, gives_rows, gives_means
        ),
        out_shape=out_shape,
        in_specs=[IN_SMEM] + [IN_VMEM] * (len(operands) - 1),
        out_specs=[IN_VMEM] * len(out_shape),
        scratch_shapes=[pltpu.VMEM(shape, jnp.bfloat16)] * 4,
        compiler_params=pltpu.CompilerParams(vmem_limit_bytes=KERNEL_VMEM),
        cost_estimate=pl.CostEstimate(
            flops=4 * rows * width * width, bytes_accessed=4 * rows * width, transcendentals=2 * rows * width
        ),
        name="stage",
    )(*operands)
    rows_out = results[0] if gives_rows else None
    means_out = results[-1] if gives_means else None
    return rows_out, means_out


def lane_groups(histories, core):
    query_count, seq_len, width = histories.shape
    lane = query_count // 2
    mine = lax.dynamic_slice_in_dim(histories, core * lane, lane, 0)
    return [
        mine[first : first + GROUP].reshape(GROUP * seq_len, width)
        for first in range(0, lane, GROUP)
    ]


def query_tower(place, injected, weight, other_weight, gain, other_gain):
    chips = lax.axis_size(SEGMENT) // 2
    groups = len(injected)
    gains = (gain, other_gain)
    gap = 2
    rows, *weights = first_stage(place, injected[0], weight, other_weight, gains)
    arriving = {gap: to_chip(rows, 1)}
    means = []
    for tick in range(1, groups + gap * (chips - 1)):
        begun = injected[tick] if tick < groups else None
        incoming = arriving.pop(tick, None)
        busy = [c for c in range(chips) if 0 <= tick - gap * c < groups]
        sends = any(c < chips - 1 for c in busy)
        ends = chips - 1 in busy
        rows, mean = stage(place, begun, incoming, weights, gains, GROUP, sends, ends)
        if sends:
            arriving[tick + gap] = to_chip(rows, 1)
        if ends:
            means.append(mean)
    return jnp.concatenate(means, axis=0)


def from_last_chip(value, chip):
    ahead, back, across = to_chip(value, 1), to_chip(value, -1), to_chip(value, 2)
    return jnp.where(
        chip == 3, value, jnp.where(chip == 0, ahead, jnp.where(chip == 2, back, across))
    )


def summed_over_segment(grads, targets, rows, chip, core):
    width = grads.shape[1]
    half, piece = rows // 2, rows // 8

    def summed(first):
        lands = targets[:, None] == first + jnp.arange(half, dtype=jnp.int32)[None, :]
        return lax.dot_general(
            lands.astype(jnp.bfloat16), grads, (((0,), (0,)), ((), ())), preferred_element_type=jnp.float32
        )

    given = to_other_core(summed((1 - core) * half).astype(jnp.bfloat16))
    part = summed(core * half) + given.astype(jnp.float32)
    rounded = part.astype(jnp.bfloat16)

    def piece_of(array, index):
        return lax.dynamic_slice_in_dim(array, (index % 4) * piece, piece, 0)

    got = [to_chip(piece_of(rounded, chip + steps), steps) for steps in (1, 2, 3)]
    total = piece_of(part, chip)
    for term in got:
        total = total + term.astype(jnp.float32)
    total = total.astype(jnp.bfloat16)
    whole = jnp.zeros((half, width), jnp.bfloat16)
    for steps, term in enumerate([total] + [to_chip(total, steps) for steps in (1, 2, 3)]):
        whole = lax.dynamic_update_slice_in_dim(whole, term, ((chip - steps) % 4) * piece, 0)
    other = to_other_core(whole)
    low = jnp.where(core == 0, whole, other)
    high = jnp.where(core == 0, other, whole)
    return jnp.concatenate([low, high], axis=0).astype(jnp.float32)


def combine(earlier, later):
    highest = jnp.maximum(earlier[0], later[0])
    summed = earlier[1] * jnp.exp(earlier[0] - highest) + later[1] * jnp.exp(later[0] - highest)
    return jnp.stack([highest, summed, earlier[2] + later[2]])


def combined_over_segment(stats):
    stats = combine(stats, to_other_core(stats))
    ahead, back, across = to_chip(stats, 1), to_chip(stats, -1), to_chip(stats, 2)
    return combine(combine(stats, across), combine(ahead, back))


def shards(
    histories,
    segment_weight,
    segment_gain,
    item_table,
    item_weight,
    query_scale,
    cand_bias,
    cand_owner,
    cand_slot,
):
    segment_idx = lax.axis_index(SEGMENT)
    chip, core = segment_idx // 2, segment_idx % 2
    shard_count = lax.axis_size(DP)
    query_count, _, model_width = histories.shape
    cand_count = cand_owner.shape[1]
    count_rows = query_count * cand_count
    capacity = 4 * count_rows // shard_count
    slots = shard_count * capacity
    item_rows = item_table.shape[0]

    owner_ids = cand_owner.reshape(-1)
    slot_ids = cand_slot.reshape(-1)
    one_hot = owner_ids[:, None] == jnp.arange(shard_count, dtype=jnp.int32)[None, :]
    before = jnp.arange(count_rows)[:, None] > jnp.arange(count_rows)[None, :]
    ranks = jnp.dot(
        before.astype(jnp.bfloat16), one_hot.astype(jnp.bfloat16), preferred_element_type=jnp.float32
    )
    within = jnp.sum(jnp.where(one_hot, ranks, 0.0), axis=1).astype(jnp.int32)
    position = owner_ids * capacity + within
    placed = position[:, None] == jnp.arange(slots, dtype=jnp.int32)[None, :]
    outbox = jnp.sum(jnp.where(placed, slot_ids[:, None] + 1, 0), axis=0)
    placed = placed.astype(jnp.bfloat16)
    inbox = lax.all_to_all(
        outbox.reshape(shard_count, capacity), DP, split_axis=0, concat_axis=0, tiled=True
    ).reshape(-1)
    wanted = (inbox[:, None] - 1 == jnp.arange(item_rows, dtype=jnp.int32)[None, :]).astype(
        jnp.bfloat16
    )
    fetched = jnp.dot(wanted, item_table, preferred_element_type=jnp.float32).astype(jnp.bfloat16)
    weight = segment_weight[0]
    other_weight = to_other_core(weight)
    weight, other_weight, histories, fetched, placed, wanted = lax.optimization_barrier(
        (weight, other_weight, histories, fetched, placed, wanted)
    )
    returned = lax.all_to_all(
        fetched.reshape(shard_count, capacity, -1), DP, split_axis=0, concat_axis=0, tiled=True
    )
    place = jnp.stack([(chip == 0).astype(jnp.int32), core.astype(jnp.int32)])
    injected = lane_groups(histories, core)
    other_gain = to_other_core(segment_gain)
    pooled = lax.cond(
        segment_idx < lax.axis_size(SEGMENT),
        query_tower,
        lambda *_: jnp.zeros((query_count // 2, model_width), jnp.float32),
        place,
        injected,
        weight,
        other_weight,
        segment_gain,
        other_gain,
    )
    returned, pooled = lax.optimization_barrier((returned, pooled))
    returned = returned.reshape(slots, -1)
    own_rows = jnp.dot(placed, returned, preferred_element_type=jnp.float32).astype(jnp.bfloat16)
    item_pre = jnp.dot(own_rows, item_weight, preferred_element_type=jnp.float32)
    logistic = jax.nn.sigmoid(item_pre)
    item_vec = (item_pre * logistic).astype(jnp.bfloat16)
    slope = logistic * (1.0 + item_pre * (1.0 - logistic))
    item_vec, slope = lax.optimization_barrier((item_vec, slope))

    lane_vec = (
        pooled * lax.rsqrt(jnp.mean(pooled * pooled, axis=-1, keepdims=True) + EPSILON)
    ).astype(jnp.bfloat16)
    lane_vec = from_last_chip(lane_vec, chip)
    other_vec = to_other_core(lane_vec)
    query_vec = jnp.concatenate(
        [jnp.where(core == 0, lane_vec, other_vec), jnp.where(core == 0, other_vec, lane_vec)],
        axis=0,
    )

    row_query = jnp.arange(count_rows, dtype=jnp.int32) // cand_count
    mine = row_query[:, None] == jnp.arange(query_count, dtype=jnp.int32)[None, :]
    products = lax.dot_general(
        item_vec, query_vec, (((1,), (1,)), ((), ())), preferred_element_type=jnp.float32
    )
    factor = query_scale[None, :] / math.sqrt(model_width)
    scores = query_scale[None, :] * products / math.sqrt(model_width) + cand_bias.reshape(-1)[:, None]
    highest = jnp.max(jnp.where(mine, scores, -jnp.inf), axis=0)
    shifted = jnp.exp(jnp.where(mine, scores - highest[None, :], -jnp.inf))
    summed = jnp.sum(shifted, axis=0)
    is_target = (jnp.arange(count_rows) % cand_count == 0)[:, None] & mine & (segment_idx == 0)
    positive = jnp.sum(jnp.where(is_target, scores, 0.0), axis=0)
    top, total, positive = combined_over_segment(jnp.stack([highest, summed, positive]))
    lse = top + jnp.log(total)
    query_loss = lse - positive

    widened = jnp.broadcast_to(
        query_vec.astype(jnp.float32)[:, None, :], (query_count, cand_count, model_width)
    ).reshape(count_rows, model_width)
    sloped = (widened * slope).astype(jnp.bfloat16)
    unscaled = lax.dot_general(
        sloped, item_weight, (((1,), (1,)), ((), ())), preferred_element_type=jnp.float32
    )
    unscaled, lse = lax.optimization_barrier((unscaled, lse))
    score_grad = jnp.exp(jnp.where(mine, scores - lse[None, :], -jnp.inf)) - is_target
    row_factor = jnp.sum(score_grad * factor, axis=1)
    row_grad = (unscaled * row_factor[:, None]).astype(jnp.bfloat16)
    grad_box = lax.dot_general(
        placed, row_grad, (((0,), (0,)), ((), ())), preferred_element_type=jnp.float32
    ).astype(jnp.bfloat16)
    got_grad = lax.all_to_all(
        grad_box.reshape(shard_count, capacity, -1), DP, split_axis=0, concat_axis=0, tiled=True
    ).reshape(slots, -1)
    table_grad = summed_over_segment(got_grad, inbox - 1, item_rows, chip, core)
    return (query_loss, table_grad)


def solution(mesh):
    return jax.shard_map(
        shards,
        mesh=mesh,
        in_specs=(
            P(DP, None, None),
            P(SEGMENT, None, None),
            P(SEGMENT, None),
            P(DP, None),
            P(),
            P(DP),
            P(DP, SEGMENT),
            P(DP, SEGMENT),
            P(DP, SEGMENT),
        ),
        out_specs=(P(DP), P(DP, None)),
        check_vma=False,
    )
```

```python
import functools
import math

import jax
import jax.numpy as jnp
from jax import lax
from jax.experimental import pallas as pl
from jax.experimental.pallas import tpu as pltpu
from jax.sharding import PartitionSpec as P

EPSILON = 1e-05
SEGMENT = "segment"
DP = "dp"
GROUP = 2
TILE = 512
KERNEL_VMEM = 12 * 2**20
IN_VMEM = pl.BlockSpec(memory_space=pltpu.VMEM)
IN_SMEM = pl.BlockSpec(memory_space=pltpu.SMEM)
ANYWHERE = pl.BlockSpec(memory_space=pl.ANY)


def to_other_core(value):
    count = lax.axis_size(SEGMENT)
    return lax.ppermute(value, SEGMENT, [(i, i ^ 1) for i in range(count)])


def to_chip(value, steps):
    count = lax.axis_size(SEGMENT)
    return lax.ppermute(value, SEGMENT, [(i, (i + 2 * steps) % count) for i in range(count)])


def column_tiles(width):
    return [pl.ds(start, TILE) for start in range(0, width, TILE)]


def layer_into(source, weight, gain, normed, target, arrivals=None):
    widened = source[...].astype(jnp.float32)
    mean_square = jnp.mean(widened * widened, axis=-1, keepdims=True)
    normed[...] = (widened * lax.rsqrt(mean_square + EPSILON) * gain[...]).astype(jnp.bfloat16)
    for k, columns in enumerate(column_tiles(target.shape[1])):
        if arrivals is not None:
            arrivals[k].wait()
        projected = jnp.dot(normed[...], weight[:, columns], preferred_element_type=jnp.float32)
        gated = projected / (1.0 + jnp.exp(-projected))
        target[:, columns] = (source[:, columns].astype(jnp.float32) + gated).astype(jnp.bfloat16)


def first_stage_kernel(
    place, injected, own_source, other_source, own_gain, other_gain,
    rows_out, own_weight, other_weight, middle, normed, sems,
):
    def arriving(source, held, first):
        return [
            pltpu.make_async_copy(source.at[:, columns], held.at[:, columns], sems.at[first + k])
            for k, columns in enumerate(column_tiles(held.shape[1]))
        ]

    own = arriving(own_source, own_weight, 0)
    other = arriving(other_source, other_weight, len(own))

    def layers(first, first_weight, first_gain, second, second_weight, second_gain):
        for copy in first + second:
            copy.start()
        layer_into(injected, first_weight, first_gain, normed, middle, first)
        layer_into(middle, second_weight, second_gain, normed, rows_out, second)

    @pl.when(place[1] == 0)
    def _():
        layers(own, own_weight, own_gain, other, other_weight, other_gain)

    @pl.when(place[1] == 1)
    def _():
        layers(other, other_weight, other_gain, own, own_weight, own_gain)


def first_stage(place, injected, weight, other_weight, gains):
    rows, width = injected.shape
    copies = 2 * len(column_tiles(width))
    return pl.pallas_call(
        first_stage_kernel,
        out_shape=[
            jax.ShapeDtypeStruct(injected.shape, jnp.bfloat16),
            pltpu.VMEM(weight.shape, weight.dtype),
            pltpu.VMEM(weight.shape, weight.dtype),
        ],
        in_specs=[IN_SMEM, IN_VMEM, ANYWHERE, ANYWHERE, IN_VMEM, IN_VMEM],
        out_specs=[IN_VMEM] * 3,
        scratch_shapes=[pltpu.VMEM(injected.shape, jnp.bfloat16)] * 2
        + [pltpu.SemaphoreType.DMA((copies,))],
        compiler_params=pltpu.CompilerParams(vmem_limit_bytes=KERNEL_VMEM),
        cost_estimate=pl.CostEstimate(
            flops=4 * rows * width * width,
            bytes_accessed=4 * width * width,
            transcendentals=2 * rows * width,
        ),
        name="first_stage",
    )(place, injected, weight, other_weight, *gains)


def stage_kernel(has_injected, has_incoming, gives_rows, gives_means, *refs):
    refs = list(refs)
    place = refs.pop(0)
    injected = refs.pop(0) if has_injected else None
    incoming = refs.pop(0) if has_incoming else None
    own_weight, other_weight, own_gain, other_gain = refs[:4]
    refs = refs[4:]
    rows_out = refs.pop(0) if gives_rows else None
    means_out = refs.pop(0) if gives_means else None
    start, middle, normed, final = refs
    if rows_out is None:
        rows_out = final
    is_first, core = place[0], place[1]
    if has_injected and has_incoming:

        @pl.when(is_first == 1)
        def _():
            start[...] = injected[...]

        @pl.when(is_first == 0)
        def _():
            start[...] = incoming[...]

        begin = start
    else:
        begin = injected if has_injected else incoming

    @pl.when(core == 0)
    def _():
        layer_into(begin, own_weight, own_gain, normed, middle)
        layer_into(middle, other_weight, other_gain, normed, rows_out)

    @pl.when(core == 1)
    def _():
        layer_into(begin, other_weight, other_gain, normed, middle)
        layer_into(middle, own_weight, own_gain, normed, rows_out)

    if gives_means:
        groups = means_out.shape[0]
        length = rows_out.shape[0] // groups
        for k in range(groups):
            tokens = rows_out[pl.ds(k * length, length), :].astype(jnp.float32)
            means_out[pl.ds(k, 1), :] = jnp.mean(tokens, axis=0, keepdims=True)


def stage(place, injected, incoming, weights, gains, groups, gives_rows, gives_means):
    shape = (injected if injected is not None else incoming).shape
    rows, width = shape
    operands = [place]
    operands += [value for value in (injected, incoming) if value is not None]
    operands += [*weights, *gains]
    out_shape = []
    if gives_rows:
        out_shape.append(jax.ShapeDtypeStruct(shape, jnp.bfloat16))
    if gives_means:
        out_shape.append(jax.ShapeDtypeStruct((groups, width), jnp.float32))
    results = pl.pallas_call(
        functools.partial(
            stage_kernel, injected is not None, incoming is not None, gives_rows, gives_means
        ),
        out_shape=out_shape,
        in_specs=[IN_SMEM] + [IN_VMEM] * (len(operands) - 1),
        out_specs=[IN_VMEM] * len(out_shape),
        scratch_shapes=[pltpu.VMEM(shape, jnp.bfloat16)] * 4,
        compiler_params=pltpu.CompilerParams(vmem_limit_bytes=KERNEL_VMEM),
        cost_estimate=pl.CostEstimate(
            flops=4 * rows * width * width, bytes_accessed=4 * rows * width, transcendentals=2 * rows * width
        ),
        name="stage",
    )(*operands)
    rows_out = results[0] if gives_rows else None
    means_out = results[-1] if gives_means else None
    return rows_out, means_out


def lane_groups(histories, core):
    query_count, seq_len, width = histories.shape
    lane = query_count // 2
    mine = lax.dynamic_slice_in_dim(histories, core * lane, lane, 0)
    return [
        mine[first : first + GROUP].reshape(GROUP * seq_len, width)
        for first in range(0, lane, GROUP)
    ]


def query_tower(place, injected, weight, other_weight, gain, other_gain):
    chips = lax.axis_size(SEGMENT) // 2
    groups = len(injected)
    gains = (gain, other_gain)
    gap = 2
    rows, *weights = first_stage(place, injected[0], weight, other_weight, gains)
    arriving = {gap: to_chip(rows, 1)}
    means = []
    for tick in range(1, groups + gap * (chips - 1)):
        begun = injected[tick] if tick < groups else None
        incoming = arriving.pop(tick, None)
        busy = [c for c in range(chips) if 0 <= tick - gap * c < groups]
        sends = any(c < chips - 1 for c in busy)
        ends = chips - 1 in busy
        rows, mean = stage(place, begun, incoming, weights, gains, GROUP, sends, ends)
        if sends:
            arriving[tick + gap] = to_chip(rows, 1)
        if ends:
            means.append(mean)
    return jnp.concatenate(means, axis=0)


def from_last_chip(value, chip):
    ahead, back, across = to_chip(value, 1), to_chip(value, -1), to_chip(value, 2)
    return jnp.where(
        chip == 3, value, jnp.where(chip == 0, ahead, jnp.where(chip == 2, back, across))
    )


def summed_over_segment(grads, targets, rows, chip, core):
    width = grads.shape[1]
    half, piece = rows // 2, rows // 8

    def summed(first):
        lands = targets[:, None] == first + jnp.arange(half, dtype=jnp.int32)[None, :]
        return lax.dot_general(
            lands.astype(jnp.bfloat16), grads, (((0,), (0,)), ((), ())), preferred_element_type=jnp.float32
        )

    given = to_other_core(summed((1 - core) * half).astype(jnp.bfloat16))
    part = summed(core * half) + given.astype(jnp.float32)
    rounded = part.astype(jnp.bfloat16)

    def piece_of(array, index):
        return lax.dynamic_slice_in_dim(array, (index % 4) * piece, piece, 0)

    got = [to_chip(piece_of(rounded, chip + steps), steps) for steps in (1, 2, 3)]
    total = piece_of(part, chip)
    for term in got:
        total = total + term.astype(jnp.float32)
    total = total.astype(jnp.bfloat16)
    whole = jnp.zeros((half, width), jnp.bfloat16)
    for steps, term in enumerate([total] + [to_chip(total, steps) for steps in (1, 2, 3)]):
        whole = lax.dynamic_update_slice_in_dim(whole, term, ((chip - steps) % 4) * piece, 0)
    other = to_other_core(whole)
    low = jnp.where(core == 0, whole, other)
    high = jnp.where(core == 0, other, whole)
    return jnp.concatenate([low, high], axis=0).astype(jnp.float32)


def combine(earlier, later):
    highest = jnp.maximum(earlier[0], later[0])
    summed = earlier[1] * jnp.exp(earlier[0] - highest) + later[1] * jnp.exp(later[0] - highest)
    return jnp.stack([highest, summed, earlier[2] + later[2]])


def combined_over_segment(stats):
    stats = combine(stats, to_other_core(stats))
    ahead, back, across = to_chip(stats, 1), to_chip(stats, -1), to_chip(stats, 2)
    return combine(combine(stats, across), combine(ahead, back))


def shards(
    histories,
    segment_weight,
    segment_gain,
    item_table,
    item_weight,
    query_scale,
    cand_bias,
    cand_owner,
    cand_slot,
):
    segment_idx = lax.axis_index(SEGMENT)
    chip, core = segment_idx // 2, segment_idx % 2
    shard_count = lax.axis_size(DP)
    query_count, _, model_width = histories.shape
    cand_count = cand_owner.shape[1]
    count_rows = query_count * cand_count
    capacity = 4 * count_rows // shard_count
    slots = shard_count * capacity
    item_rows = item_table.shape[0]

    owner_ids = cand_owner.reshape(-1)
    slot_ids = cand_slot.reshape(-1)
    one_hot = owner_ids[:, None] == jnp.arange(shard_count, dtype=jnp.int32)[None, :]
    before = jnp.arange(count_rows)[:, None] > jnp.arange(count_rows)[None, :]
    ranks = jnp.dot(
        before.astype(jnp.bfloat16), one_hot.astype(jnp.bfloat16), preferred_element_type=jnp.float32
    )
    within = jnp.sum(jnp.where(one_hot, ranks, 0.0), axis=1).astype(jnp.int32)
    position = owner_ids * capacity + within
    placed = position[:, None] == jnp.arange(slots, dtype=jnp.int32)[None, :]
    outbox = jnp.sum(jnp.where(placed, slot_ids[:, None] + 1, 0), axis=0)
    placed = placed.astype(jnp.bfloat16)
    inbox = lax.all_to_all(
        outbox.reshape(shard_count, capacity), DP, split_axis=0, concat_axis=0, tiled=True
    ).reshape(-1)
    wanted = (inbox[:, None] - 1 == jnp.arange(item_rows, dtype=jnp.int32)[None, :]).astype(
        jnp.bfloat16
    )
    fetched = jnp.dot(wanted, item_table, preferred_element_type=jnp.float32).astype(jnp.bfloat16)
    weight = segment_weight[0]
    other_weight = to_other_core(weight)
    other_gain = to_other_core(segment_gain)
    injected = lane_groups(histories, core)
    weight, other_weight, other_gain, injected, fetched, placed = lax.optimization_barrier(
        (weight, other_weight, other_gain, injected, fetched, placed)
    )
    returned = lax.all_to_all(
        fetched.reshape(shard_count, capacity, -1), DP, split_axis=0, concat_axis=0, tiled=True
    )
    place = jnp.stack([(chip == 0).astype(jnp.int32), core.astype(jnp.int32)])
    pooled = lax.cond(
        segment_idx < lax.axis_size(SEGMENT),
        query_tower,
        lambda *_: jnp.zeros((query_count // 2, model_width), jnp.float32),
        place,
        injected,
        weight,
        other_weight,
        segment_gain,
        other_gain,
    )
    returned, pooled = lax.optimization_barrier((returned, pooled))
    returned = returned.reshape(slots, -1)
    own_rows = jnp.dot(placed, returned, preferred_element_type=jnp.float32).astype(jnp.bfloat16)
    item_pre = jnp.dot(own_rows, item_weight, preferred_element_type=jnp.float32)
    logistic = jax.nn.sigmoid(item_pre)
    item_vec = (item_pre * logistic).astype(jnp.bfloat16)
    slope = logistic * (1.0 + item_pre * (1.0 - logistic))

    lane_vec = (
        pooled * lax.rsqrt(jnp.mean(pooled * pooled, axis=-1, keepdims=True) + EPSILON)
    ).astype(jnp.bfloat16)
    lane_vec = from_last_chip(lane_vec, chip)
    lane_vec, item_vec, slope = lax.optimization_barrier((lane_vec, item_vec, slope))
    other_vec = to_other_core(lane_vec)
    query_vec = jnp.concatenate(
        [jnp.where(core == 0, lane_vec, other_vec), jnp.where(core == 0, other_vec, lane_vec)],
        axis=0,
    )

    row_query = jnp.arange(count_rows, dtype=jnp.int32) // cand_count
    mine = row_query[:, None] == jnp.arange(query_count, dtype=jnp.int32)[None, :]
    products = lax.dot_general(
        item_vec, query_vec, (((1,), (1,)), ((), ())), preferred_element_type=jnp.float32
    )
    factor = query_scale[None, :] / math.sqrt(model_width)
    scores = query_scale[None, :] * products / math.sqrt(model_width) + cand_bias.reshape(-1)[:, None]
    highest = jnp.max(jnp.where(mine, scores, -jnp.inf), axis=0)
    shifted = jnp.exp(jnp.where(mine, scores - highest[None, :], -jnp.inf))
    summed = jnp.sum(shifted, axis=0)
    is_target = (jnp.arange(count_rows) % cand_count == 0)[:, None] & mine & (segment_idx == 0)
    positive = jnp.sum(jnp.where(is_target, scores, 0.0), axis=0)
    top, total, positive = combined_over_segment(jnp.stack([highest, summed, positive]))
    lse = top + jnp.log(total)
    query_loss = lse - positive

    widened = jnp.broadcast_to(
        query_vec.astype(jnp.float32)[:, None, :], (query_count, cand_count, model_width)
    ).reshape(count_rows, model_width)
    sloped = (widened * slope).astype(jnp.bfloat16)
    unscaled = lax.dot_general(
        sloped, item_weight, (((1,), (1,)), ((), ())), preferred_element_type=jnp.float32
    )
    unscaled, lse = lax.optimization_barrier((unscaled, lse))
    score_grad = jnp.exp(jnp.where(mine, scores - lse[None, :], -jnp.inf)) - is_target
    row_factor = jnp.sum(score_grad * factor, axis=1)
    row_grad = (unscaled * row_factor[:, None]).astype(jnp.bfloat16)
    grad_box = lax.dot_general(
        placed, row_grad, (((0,), (0,)), ((), ())), preferred_element_type=jnp.float32
    ).astype(jnp.bfloat16)
    got_grad = lax.all_to_all(
        grad_box.reshape(shard_count, capacity, -1), DP, split_axis=0, concat_axis=0, tiled=True
    ).reshape(slots, -1)
    table_grad = summed_over_segment(got_grad, inbox - 1, item_rows, chip, core)
    return (query_loss, table_grad)


def solution(mesh):
    return jax.shard_map(
        shards,
        mesh=mesh,
        in_specs=(
            P(DP, None, None),
            P(SEGMENT, None, None),
            P(SEGMENT, None),
            P(DP, None),
            P(),
            P(DP),
            P(DP, SEGMENT),
            P(DP, SEGMENT),
            P(DP, SEGMENT),
        ),
        out_specs=(P(DP), P(DP, None)),
        check_vma=False,
    )
```

```python
import functools
import math

import jax
import jax.numpy as jnp
from jax import lax
from jax.experimental import pallas as pl
from jax.experimental.pallas import tpu as pltpu
from jax.sharding import PartitionSpec as P

EPSILON = 1e-05
SEGMENT = "segment"
DP = "dp"
GROUP = 2
TILE = 512
KERNEL_VMEM = 12 * 2**20
IN_VMEM = pl.BlockSpec(memory_space=pltpu.VMEM)
IN_SMEM = pl.BlockSpec(memory_space=pltpu.SMEM)
ANYWHERE = pl.BlockSpec(memory_space=pl.ANY)


def to_other_core(value):
    count = lax.axis_size(SEGMENT)
    return lax.ppermute(value, SEGMENT, [(i, i ^ 1) for i in range(count)])


def to_chip(value, steps):
    count = lax.axis_size(SEGMENT)
    return lax.ppermute(value, SEGMENT, [(i, (i + 2 * steps) % count) for i in range(count)])


def column_tiles(width):
    return [pl.ds(start, TILE) for start in range(0, width, TILE)]


def layer_into(source, weight, gain, normed, target, arrivals=None):
    widened = source[...].astype(jnp.float32)
    mean_square = jnp.mean(widened * widened, axis=-1, keepdims=True)
    normed[...] = (widened * lax.rsqrt(mean_square + EPSILON) * gain[...]).astype(jnp.bfloat16)
    for k, columns in enumerate(column_tiles(target.shape[1])):
        if arrivals is not None:
            arrivals[k].wait()
        projected = jnp.dot(normed[...], weight[:, columns], preferred_element_type=jnp.float32)
        gated = projected / (1.0 + jnp.exp(-projected))
        target[:, columns] = (source[:, columns].astype(jnp.float32) + gated).astype(jnp.bfloat16)


def first_stage_kernel(
    place, injected, own_source, other_source, own_gain, other_gain,
    rows_out, own_weight, other_weight, middle, normed, sems,
):
    def arriving(source, held, first):
        return [
            pltpu.make_async_copy(source.at[:, columns], held.at[:, columns], sems.at[first + k])
            for k, columns in enumerate(column_tiles(held.shape[1]))
        ]

    own = arriving(own_source, own_weight, 0)
    other = arriving(other_source, other_weight, len(own))

    def layers(first, first_weight, first_gain, second, second_weight, second_gain):
        for copy in first + second:
            copy.start()
        layer_into(injected, first_weight, first_gain, normed, middle, first)
        layer_into(middle, second_weight, second_gain, normed, rows_out, second)

    @pl.when(place[1] == 0)
    def _():
        layers(own, own_weight, own_gain, other, other_weight, other_gain)

    @pl.when(place[1] == 1)
    def _():
        layers(other, other_weight, other_gain, own, own_weight, own_gain)


def first_stage(place, injected, weight, other_weight, gains):
    rows, width = injected.shape
    copies = 2 * len(column_tiles(width))
    return pl.pallas_call(
        first_stage_kernel,
        out_shape=[
            jax.ShapeDtypeStruct(injected.shape, jnp.bfloat16),
            pltpu.VMEM(weight.shape, weight.dtype),
            pltpu.VMEM(weight.shape, weight.dtype),
        ],
        in_specs=[IN_SMEM, IN_VMEM, ANYWHERE, ANYWHERE, IN_VMEM, IN_VMEM],
        out_specs=[IN_VMEM] * 3,
        scratch_shapes=[pltpu.VMEM(injected.shape, jnp.bfloat16)] * 2
        + [pltpu.SemaphoreType.DMA((copies,))],
        compiler_params=pltpu.CompilerParams(vmem_limit_bytes=KERNEL_VMEM),
        cost_estimate=pl.CostEstimate(
            flops=4 * rows * width * width,
            bytes_accessed=4 * width * width,
            transcendentals=2 * rows * width,
        ),
        name="first_stage",
    )(place, injected, weight, other_weight, *gains)


def stage_kernel(has_injected, has_incoming, gives_rows, gives_means, *refs):
    refs = list(refs)
    place = refs.pop(0)
    injected = refs.pop(0) if has_injected else None
    incoming = refs.pop(0) if has_incoming else None
    own_weight, other_weight, own_gain, other_gain = refs[:4]
    refs = refs[4:]
    rows_out = refs.pop(0) if gives_rows else None
    means_out = refs.pop(0) if gives_means else None
    start, middle, normed, final = refs
    if rows_out is None:
        rows_out = final
    is_first, core = place[0], place[1]
    if has_injected and has_incoming:

        @pl.when(is_first == 1)
        def _():
            start[...] = injected[...]

        @pl.when(is_first == 0)
        def _():
            start[...] = incoming[...]

        begin = start
    else:
        begin = injected if has_injected else incoming

    @pl.when(core == 0)
    def _():
        layer_into(begin, own_weight, own_gain, normed, middle)
        layer_into(middle, other_weight, other_gain, normed, rows_out)

    @pl.when(core == 1)
    def _():
        layer_into(begin, other_weight, other_gain, normed, middle)
        layer_into(middle, own_weight, own_gain, normed, rows_out)

    if gives_means:
        groups = means_out.shape[0]
        length = rows_out.shape[0] // groups
        for k in range(groups):
            tokens = rows_out[pl.ds(k * length, length), :].astype(jnp.float32)
            means_out[pl.ds(k, 1), :] = jnp.mean(tokens, axis=0, keepdims=True)


def stage(place, injected, incoming, weights, gains, groups, gives_rows, gives_means):
    shape = (injected if injected is not None else incoming).shape
    rows, width = shape
    operands = [place]
    operands += [value for value in (injected, incoming) if value is not None]
    operands += [*weights, *gains]
    out_shape = []
    if gives_rows:
        out_shape.append(jax.ShapeDtypeStruct(shape, jnp.bfloat16))
    if gives_means:
        out_shape.append(jax.ShapeDtypeStruct((groups, width), jnp.float32))
    results = pl.pallas_call(
        functools.partial(
            stage_kernel, injected is not None, incoming is not None, gives_rows, gives_means
        ),
        out_shape=out_shape,
        in_specs=[IN_SMEM] + [IN_VMEM] * (len(operands) - 1),
        out_specs=[IN_VMEM] * len(out_shape),
        scratch_shapes=[pltpu.VMEM(shape, jnp.bfloat16)] * 4,
        compiler_params=pltpu.CompilerParams(vmem_limit_bytes=KERNEL_VMEM),
        cost_estimate=pl.CostEstimate(
            flops=4 * rows * width * width, bytes_accessed=4 * rows * width, transcendentals=2 * rows * width
        ),
        name="stage",
    )(*operands)
    rows_out = results[0] if gives_rows else None
    means_out = results[-1] if gives_means else None
    return rows_out, means_out


def lane_groups(histories, core):
    query_count, seq_len, width = histories.shape
    lane = query_count // 2
    mine = lax.dynamic_slice_in_dim(histories, core * lane, lane, 0)
    return [
        mine[first : first + GROUP].reshape(GROUP * seq_len, width)
        for first in range(0, lane, GROUP)
    ]


def query_tower(place, injected, weight, other_weight, gain, other_gain):
    chips = lax.axis_size(SEGMENT) // 2
    groups = len(injected)
    gains = (gain, other_gain)
    gap = 2
    rows, *weights = first_stage(place, injected[0], weight, other_weight, gains)
    arriving = {gap: to_chip(rows, 1)}
    means = []
    for tick in range(1, groups + gap * (chips - 1)):
        begun = injected[tick] if tick < groups else None
        incoming = arriving.pop(tick, None)
        busy = [c for c in range(chips) if 0 <= tick - gap * c < groups]
        sends = any(c < chips - 1 for c in busy)
        ends = chips - 1 in busy
        rows, mean = stage(place, begun, incoming, weights, gains, GROUP, sends, ends)
        if sends:
            arriving[tick + gap] = to_chip(rows, 1)
        if ends:
            means.append(mean)
    return jnp.concatenate(means, axis=0)


def from_last_chip(value, chip):
    ahead, back, across = to_chip(value, 1), to_chip(value, -1), to_chip(value, 2)
    return jnp.where(
        chip == 3, value, jnp.where(chip == 0, ahead, jnp.where(chip == 2, back, across))
    )


def summed_over_segment(grads, targets, rows, chip, core):
    width = grads.shape[1]
    half, piece = rows // 2, rows // 8

    def summed(first):
        lands = targets[:, None] == first + jnp.arange(half, dtype=jnp.int32)[None, :]
        return lax.dot_general(
            lands.astype(jnp.bfloat16), grads, (((0,), (0,)), ((), ())), preferred_element_type=jnp.float32
        )

    given = to_other_core(summed((1 - core) * half).astype(jnp.bfloat16))
    part = summed(core * half) + given.astype(jnp.float32)
    rounded = part.astype(jnp.bfloat16)

    def piece_of(array, index):
        return lax.dynamic_slice_in_dim(array, (index % 4) * piece, piece, 0)

    got = [to_chip(piece_of(rounded, chip + steps), steps) for steps in (1, 2, 3)]
    total = piece_of(part, chip)
    for term in got:
        total = total + term.astype(jnp.float32)
    total = total.astype(jnp.bfloat16)
    whole = jnp.zeros((half, width), jnp.bfloat16)
    for steps, term in enumerate([total] + [to_chip(total, steps) for steps in (1, 2, 3)]):
        whole = lax.dynamic_update_slice_in_dim(whole, term, ((chip - steps) % 4) * piece, 0)
    other = to_other_core(whole)
    low = jnp.where(core == 0, whole, other)
    high = jnp.where(core == 0, other, whole)
    return jnp.concatenate([low, high], axis=0).astype(jnp.float32)


def combine(earlier, later):
    highest = jnp.maximum(earlier[0], later[0])
    summed = earlier[1] * jnp.exp(earlier[0] - highest) + later[1] * jnp.exp(later[0] - highest)
    return jnp.stack([highest, summed, earlier[2] + later[2]])


def combined_over_segment(stats):
    stats = combine(stats, to_other_core(stats))
    ahead, back, across = to_chip(stats, 1), to_chip(stats, -1), to_chip(stats, 2)
    return combine(combine(stats, across), combine(ahead, back))


def shards(
    histories,
    segment_weight,
    segment_gain,
    item_table,
    item_weight,
    query_scale,
    cand_bias,
    cand_owner,
    cand_slot,
):
    segment_idx = lax.axis_index(SEGMENT)
    chip, core = segment_idx // 2, segment_idx % 2
    shard_count = lax.axis_size(DP)
    query_count, _, model_width = histories.shape
    cand_count = cand_owner.shape[1]
    count_rows = query_count * cand_count
    capacity = 4 * count_rows // shard_count
    slots = shard_count * capacity
    item_rows = item_table.shape[0]

    owner_ids = cand_owner.reshape(-1)
    slot_ids = cand_slot.reshape(-1)
    one_hot = owner_ids[:, None] == jnp.arange(shard_count, dtype=jnp.int32)[None, :]
    before = jnp.arange(count_rows)[:, None] > jnp.arange(count_rows)[None, :]
    ranks = jnp.dot(
        before.astype(jnp.bfloat16), one_hot.astype(jnp.bfloat16), preferred_element_type=jnp.float32
    )
    within = jnp.sum(jnp.where(one_hot, ranks, 0.0), axis=1).astype(jnp.int32)
    position = owner_ids * capacity + within
    placed = position[:, None] == jnp.arange(slots, dtype=jnp.int32)[None, :]
    ranked = within[:, None] == jnp.arange(capacity, dtype=jnp.int32)[None, :]
    high, low = (slot_ids + 1) // 32, (slot_ids + 1) % 32
    parts = jnp.concatenate(
        [jnp.where(ranked, high[:, None], 0), jnp.where(ranked, low[:, None], 0)], axis=1
    )
    boxes = lax.dot_general(
        one_hot.astype(jnp.bfloat16),
        parts.astype(jnp.bfloat16),
        (((0,), (0,)), ((), ())),
        preferred_element_type=jnp.float32,
    ).astype(jnp.int32)
    outbox = boxes[:, :capacity] * 32 + boxes[:, capacity:]
    placed = placed.astype(jnp.bfloat16)
    inbox = lax.all_to_all(
        outbox, DP, split_axis=0, concat_axis=0, tiled=True
    ).reshape(-1)
    wanted = (inbox[:, None] - 1 == jnp.arange(item_rows, dtype=jnp.int32)[None, :]).astype(
        jnp.bfloat16
    )
    fetched = jnp.dot(wanted, item_table, preferred_element_type=jnp.float32).astype(jnp.bfloat16)
    weight = segment_weight[0]
    other_weight = to_other_core(weight)
    other_gain = to_other_core(segment_gain)
    injected = lane_groups(histories, core)
    weight, other_weight, other_gain, injected, fetched, placed = lax.optimization_barrier(
        (weight, other_weight, other_gain, injected, fetched, placed)
    )
    returned = lax.all_to_all(
        fetched.reshape(shard_count, capacity, -1), DP, split_axis=0, concat_axis=0, tiled=True
    )
    place = jnp.stack([(chip == 0).astype(jnp.int32), core.astype(jnp.int32)])
    pooled = lax.cond(
        segment_idx < lax.axis_size(SEGMENT),
        query_tower,
        lambda *_: jnp.zeros((query_count // 2, model_width), jnp.float32),
        place,
        injected,
        weight,
        other_weight,
        segment_gain,
        other_gain,
    )
    returned, pooled = lax.optimization_barrier((returned, pooled))
    returned = returned.reshape(slots, -1)
    own_rows = jnp.dot(placed, returned, preferred_element_type=jnp.float32).astype(jnp.bfloat16)
    item_pre = jnp.dot(own_rows, item_weight, preferred_element_type=jnp.float32)
    logistic = jax.nn.sigmoid(item_pre)
    item_vec = (item_pre * logistic).astype(jnp.bfloat16)
    slope = logistic * (1.0 + item_pre * (1.0 - logistic))

    lane_vec = (
        pooled * lax.rsqrt(jnp.mean(pooled * pooled, axis=-1, keepdims=True) + EPSILON)
    ).astype(jnp.bfloat16)
    lane_vec = from_last_chip(lane_vec, chip)
    lane_vec, item_vec, slope = lax.optimization_barrier((lane_vec, item_vec, slope))
    other_vec = to_other_core(lane_vec)
    query_vec = jnp.concatenate(
        [jnp.where(core == 0, lane_vec, other_vec), jnp.where(core == 0, other_vec, lane_vec)],
        axis=0,
    )

    row_query = jnp.arange(count_rows, dtype=jnp.int32) // cand_count
    mine = row_query[:, None] == jnp.arange(query_count, dtype=jnp.int32)[None, :]
    products = lax.dot_general(
        item_vec, query_vec, (((1,), (1,)), ((), ())), preferred_element_type=jnp.float32
    )
    factor = query_scale[None, :] / math.sqrt(model_width)
    scores = query_scale[None, :] * products / math.sqrt(model_width) + cand_bias.reshape(-1)[:, None]
    highest = jnp.max(jnp.where(mine, scores, -jnp.inf), axis=0)
    shifted = jnp.exp(jnp.where(mine, scores - highest[None, :], -jnp.inf))
    summed = jnp.sum(shifted, axis=0)
    is_target = (jnp.arange(count_rows) % cand_count == 0)[:, None] & mine & (segment_idx == 0)
    positive = jnp.sum(jnp.where(is_target, scores, 0.0), axis=0)
    top, total, positive = combined_over_segment(jnp.stack([highest, summed, positive]))
    lse = top + jnp.log(total)
    query_loss = lse - positive

    widened = jnp.broadcast_to(
        query_vec.astype(jnp.float32)[:, None, :], (query_count, cand_count, model_width)
    ).reshape(count_rows, model_width)
    sloped = (widened * slope).astype(jnp.bfloat16)
    unscaled = lax.dot_general(
        sloped, item_weight, (((1,), (1,)), ((), ())), preferred_element_type=jnp.float32
    )
    unscaled, lse = lax.optimization_barrier((unscaled, lse))
    score_grad = jnp.exp(jnp.where(mine, scores - lse[None, :], -jnp.inf)) - is_target
    row_factor = jnp.sum(score_grad * factor, axis=1)
    row_grad = (unscaled * row_factor[:, None]).astype(jnp.bfloat16)
    grad_box = lax.dot_general(
        placed, row_grad, (((0,), (0,)), ((), ())), preferred_element_type=jnp.float32
    ).astype(jnp.bfloat16)
    got_grad = lax.all_to_all(
        grad_box.reshape(shard_count, capacity, -1), DP, split_axis=0, concat_axis=0, tiled=True
    ).reshape(slots, -1)
    table_grad = summed_over_segment(got_grad, inbox - 1, item_rows, chip, core)
    return (query_loss, table_grad)


def solution(mesh):
    return jax.shard_map(
        shards,
        mesh=mesh,
        in_specs=(
            P(DP, None, None),
            P(SEGMENT, None, None),
            P(SEGMENT, None),
            P(DP, None),
            P(),
            P(DP),
            P(DP, SEGMENT),
            P(DP, SEGMENT),
            P(DP, SEGMENT),
        ),
        out_specs=(P(DP), P(DP, None)),
        check_vma=False,
    )
```

```python
import functools
import math

import jax
import jax.numpy as jnp
from jax import lax
from jax.experimental import pallas as pl
from jax.experimental.pallas import tpu as pltpu
from jax.sharding import PartitionSpec as P

EPSILON = 1e-05
SEGMENT = "segment"
DP = "dp"
GROUP = 2
TILE = 512
KERNEL_VMEM = 12 * 2**20
IN_VMEM = pl.BlockSpec(memory_space=pltpu.VMEM)
IN_SMEM = pl.BlockSpec(memory_space=pltpu.SMEM)
ANYWHERE = pl.BlockSpec(memory_space=pl.ANY)


def to_other_core(value):
    count = lax.axis_size(SEGMENT)
    return lax.ppermute(value, SEGMENT, [(i, i ^ 1) for i in range(count)])


def to_chip(value, steps):
    count = lax.axis_size(SEGMENT)
    return lax.ppermute(value, SEGMENT, [(i, (i + 2 * steps) % count) for i in range(count)])


def column_tiles(width):
    return [pl.ds(start, TILE) for start in range(0, width, TILE)]


def layer_into(source, weight, gain, normed, target, arrivals=None):
    widened = source[...].astype(jnp.float32)
    mean_square = jnp.mean(widened * widened, axis=-1, keepdims=True)
    normed[...] = (widened * lax.rsqrt(mean_square + EPSILON) * gain[...]).astype(jnp.bfloat16)
    for k, columns in enumerate(column_tiles(target.shape[1])):
        if arrivals is not None:
            arrivals[k].wait()
        projected = jnp.dot(normed[...], weight[:, columns], preferred_element_type=jnp.float32)
        gated = projected / (1.0 + jnp.exp(-projected))
        target[:, columns] = (source[:, columns].astype(jnp.float32) + gated).astype(jnp.bfloat16)


def first_stage_kernel(
    place, injected, own_source, other_source, own_gain, other_gain,
    rows_out, own_weight, other_weight, middle, normed, sems,
):
    def arriving(source, held, first):
        return [
            pltpu.make_async_copy(source.at[:, columns], held.at[:, columns], sems.at[first + k])
            for k, columns in enumerate(column_tiles(held.shape[1]))
        ]

    own = arriving(own_source, own_weight, 0)
    other = arriving(other_source, other_weight, len(own))

    def layers(first, first_weight, first_gain, second, second_weight, second_gain):
        for copy in first + second:
            copy.start()
        layer_into(injected, first_weight, first_gain, normed, middle, first)
        layer_into(middle, second_weight, second_gain, normed, rows_out, second)

    @pl.when(place[1] == 0)
    def _():
        layers(own, own_weight, own_gain, other, other_weight, other_gain)

    @pl.when(place[1] == 1)
    def _():
        layers(other, other_weight, other_gain, own, own_weight, own_gain)


def first_stage(place, injected, weight, other_weight, gains):
    rows, width = injected.shape
    copies = 2 * len(column_tiles(width))
    return pl.pallas_call(
        first_stage_kernel,
        out_shape=[
            jax.ShapeDtypeStruct(injected.shape, jnp.bfloat16),
            pltpu.VMEM(weight.shape, weight.dtype),
            pltpu.VMEM(weight.shape, weight.dtype),
        ],
        in_specs=[IN_SMEM, IN_VMEM, ANYWHERE, ANYWHERE, IN_VMEM, IN_VMEM],
        out_specs=[IN_VMEM] * 3,
        scratch_shapes=[pltpu.VMEM(injected.shape, jnp.bfloat16)] * 2
        + [pltpu.SemaphoreType.DMA((copies,))],
        compiler_params=pltpu.CompilerParams(vmem_limit_bytes=KERNEL_VMEM),
        cost_estimate=pl.CostEstimate(
            flops=4 * rows * width * width,
            bytes_accessed=4 * width * width,
            transcendentals=2 * rows * width,
        ),
        name="first_stage",
    )(place, injected, weight, other_weight, *gains)


def stage_kernel(has_injected, has_incoming, gives_rows, gives_means, *refs):
    refs = list(refs)
    place = refs.pop(0)
    injected = refs.pop(0) if has_injected else None
    incoming = refs.pop(0) if has_incoming else None
    own_weight, other_weight, own_gain, other_gain = refs[:4]
    refs = refs[4:]
    rows_out = refs.pop(0) if gives_rows else None
    means_out = refs.pop(0) if gives_means else None
    start, middle, normed, final = refs
    if rows_out is None:
        rows_out = final
    is_first, core = place[0], place[1]
    if has_injected and has_incoming:

        @pl.when(is_first == 1)
        def _():
            start[...] = injected[...]

        @pl.when(is_first == 0)
        def _():
            start[...] = incoming[...]

        begin = start
    else:
        begin = injected if has_injected else incoming

    @pl.when(core == 0)
    def _():
        layer_into(begin, own_weight, own_gain, normed, middle)
        layer_into(middle, other_weight, other_gain, normed, rows_out)

    @pl.when(core == 1)
    def _():
        layer_into(begin, other_weight, other_gain, normed, middle)
        layer_into(middle, own_weight, own_gain, normed, rows_out)

    if gives_means:
        groups = means_out.shape[0]
        length = rows_out.shape[0] // groups
        for k in range(groups):
            tokens = rows_out[pl.ds(k * length, length), :].astype(jnp.float32)
            means_out[pl.ds(k, 1), :] = jnp.mean(tokens, axis=0, keepdims=True)


def stage(place, injected, incoming, weights, gains, groups, gives_rows, gives_means):
    shape = (injected if injected is not None else incoming).shape
    rows, width = shape
    operands = [place]
    operands += [value for value in (injected, incoming) if value is not None]
    operands += [*weights, *gains]
    out_shape = []
    if gives_rows:
        out_shape.append(jax.ShapeDtypeStruct(shape, jnp.bfloat16))
    if gives_means:
        out_shape.append(jax.ShapeDtypeStruct((groups, width), jnp.float32))
    results = pl.pallas_call(
        functools.partial(
            stage_kernel, injected is not None, incoming is not None, gives_rows, gives_means
        ),
        out_shape=out_shape,
        in_specs=[IN_SMEM] + [IN_VMEM] * (len(operands) - 1),
        out_specs=[IN_VMEM] * len(out_shape),
        scratch_shapes=[pltpu.VMEM(shape, jnp.bfloat16)] * 4,
        compiler_params=pltpu.CompilerParams(vmem_limit_bytes=KERNEL_VMEM),
        cost_estimate=pl.CostEstimate(
            flops=4 * rows * width * width, bytes_accessed=4 * rows * width, transcendentals=2 * rows * width
        ),
        name="stage",
    )(*operands)
    rows_out = results[0] if gives_rows else None
    means_out = results[-1] if gives_means else None
    return rows_out, means_out


def lane_groups(histories, core):
    query_count, seq_len, width = histories.shape
    lane = query_count // 2
    mine = lax.dynamic_slice_in_dim(histories, core * lane, lane, 0)
    return [
        mine[first : first + GROUP].reshape(GROUP * seq_len, width)
        for first in range(0, lane, GROUP)
    ]


def query_tower(place, injected, weight, other_weight, gain, other_gain):
    chips = lax.axis_size(SEGMENT) // 2
    groups = len(injected)
    gains = (gain, other_gain)
    gap = 2
    rows, *weights = first_stage(place, injected[0], weight, other_weight, gains)
    arriving = {gap: to_chip(rows, 1)}
    means = []
    for tick in range(1, groups + gap * (chips - 1)):
        begun = injected[tick] if tick < groups else None
        incoming = arriving.pop(tick, None)
        busy = [c for c in range(chips) if 0 <= tick - gap * c < groups]
        sends = any(c < chips - 1 for c in busy)
        ends = chips - 1 in busy
        rows, mean = stage(place, begun, incoming, weights, gains, GROUP, sends, ends)
        if sends:
            arriving[tick + gap] = to_chip(rows, 1)
        if ends:
            means.append(mean)
    return jnp.concatenate(means, axis=0)


def from_last_chip(value, chip):
    ahead, back, across = to_chip(value, 1), to_chip(value, -1), to_chip(value, 2)
    return jnp.where(
        chip == 3, value, jnp.where(chip == 0, ahead, jnp.where(chip == 2, back, across))
    )


def summed_over_segment(grads, targets, rows, chip, core):
    width = grads.shape[1]
    half, piece = rows // 2, rows // 8

    def summed(first):
        lands = targets[:, None] == first + jnp.arange(half, dtype=jnp.int32)[None, :]
        return lax.dot_general(
            lands.astype(jnp.bfloat16), grads, (((0,), (0,)), ((), ())), preferred_element_type=jnp.float32
        )

    given = to_other_core(summed((1 - core) * half).astype(jnp.bfloat16))
    part = summed(core * half) + given.astype(jnp.float32)
    rounded = part.astype(jnp.bfloat16)

    def piece_of(array, index):
        return lax.dynamic_slice_in_dim(array, (index % 4) * piece, piece, 0)

    got = [to_chip(piece_of(rounded, chip + steps), steps) for steps in (1, 2, 3)]
    total = piece_of(part, chip)
    for term in got:
        total = total + term.astype(jnp.float32)
    total = total.astype(jnp.bfloat16)
    whole = jnp.zeros((half, width), jnp.bfloat16)
    for steps, term in enumerate([total] + [to_chip(total, steps) for steps in (1, 2, 3)]):
        whole = lax.dynamic_update_slice_in_dim(whole, term, ((chip - steps) % 4) * piece, 0)
    other = to_other_core(whole)
    low = jnp.where(core == 0, whole, other)
    high = jnp.where(core == 0, other, whole)
    return jnp.concatenate([low, high], axis=0).astype(jnp.float32)


def combine(earlier, later):
    highest = jnp.maximum(earlier[0], later[0])
    summed = earlier[1] * jnp.exp(earlier[0] - highest) + later[1] * jnp.exp(later[0] - highest)
    return jnp.stack([highest, summed, earlier[2] + later[2]])


def combined_over_segment(stats):
    stats = combine(stats, to_other_core(stats))
    ahead, back, across = to_chip(stats, 1), to_chip(stats, -1), to_chip(stats, 2)
    return combine(combine(stats, across), combine(ahead, back))


def shards(
    histories,
    segment_weight,
    segment_gain,
    item_table,
    item_weight,
    query_scale,
    cand_bias,
    cand_owner,
    cand_slot,
):
    segment_idx = lax.axis_index(SEGMENT)
    chip, core = segment_idx // 2, segment_idx % 2
    shard_count = lax.axis_size(DP)
    query_count, _, model_width = histories.shape
    cand_count = cand_owner.shape[1]
    count_rows = query_count * cand_count
    capacity = 4 * count_rows // shard_count
    slots = shard_count * capacity
    item_rows = item_table.shape[0]

    owner_ids = cand_owner.reshape(-1)
    slot_ids = cand_slot.reshape(-1)
    one_hot = owner_ids[:, None] == jnp.arange(shard_count, dtype=jnp.int32)[None, :]
    before = jnp.arange(count_rows)[:, None] > jnp.arange(count_rows)[None, :]
    ranks = jnp.dot(
        before.astype(jnp.bfloat16), one_hot.astype(jnp.bfloat16), preferred_element_type=jnp.float32
    )
    within = jnp.sum(jnp.where(one_hot, ranks, 0.0), axis=1).astype(jnp.int32)
    position = owner_ids * capacity + within
    placed = position[:, None] == jnp.arange(slots, dtype=jnp.int32)[None, :]
    ranked = within[:, None] == jnp.arange(capacity, dtype=jnp.int32)[None, :]
    high, low = (slot_ids + 1) // 32, (slot_ids + 1) % 32
    parts = jnp.concatenate(
        [jnp.where(ranked, high[:, None], 0), jnp.where(ranked, low[:, None], 0)], axis=1
    )
    boxes = lax.dot_general(
        one_hot.astype(jnp.bfloat16),
        parts.astype(jnp.bfloat16),
        (((0,), (0,)), ((), ())),
        preferred_element_type=jnp.float32,
    ).astype(jnp.int32)
    outbox = boxes[:, :capacity] * 32 + boxes[:, capacity:]
    placed = placed.astype(jnp.bfloat16)
    inbox = lax.all_to_all(
        outbox, DP, split_axis=0, concat_axis=0, tiled=True
    ).reshape(-1)
    wanted = (jnp.arange(item_rows, dtype=jnp.int32)[:, None] == inbox[None, :] - 1).astype(
        jnp.bfloat16
    )
    fetched = lax.dot_general(
        wanted, item_table, (((0,), (0,)), ((), ())), preferred_element_type=jnp.float32
    ).astype(jnp.bfloat16)
    weight = segment_weight[0]
    other_weight = to_other_core(weight)
    other_gain = to_other_core(segment_gain)
    injected = lane_groups(histories, core)
    weight, other_weight, other_gain, injected, fetched, placed = lax.optimization_barrier(
        (weight, other_weight, other_gain, injected, fetched, placed)
    )
    returned = lax.all_to_all(
        fetched.reshape(shard_count, capacity, -1), DP, split_axis=0, concat_axis=0, tiled=True
    )
    place = jnp.stack([(chip == 0).astype(jnp.int32), core.astype(jnp.int32)])
    pooled = lax.cond(
        segment_idx < lax.axis_size(SEGMENT),
        query_tower,
        lambda *_: jnp.zeros((query_count // 2, model_width), jnp.float32),
        place,
        injected,
        weight,
        other_weight,
        segment_gain,
        other_gain,
    )
    returned, pooled = lax.optimization_barrier((returned, pooled))
    returned = returned.reshape(slots, -1)
    own_rows = jnp.dot(placed, returned, preferred_element_type=jnp.float32).astype(jnp.bfloat16)
    item_pre = jnp.dot(own_rows, item_weight, preferred_element_type=jnp.float32)
    logistic = jax.nn.sigmoid(item_pre)
    item_vec = (item_pre * logistic).astype(jnp.bfloat16)
    slope = logistic * (1.0 + item_pre * (1.0 - logistic))

    lane_vec = (
        pooled * lax.rsqrt(jnp.mean(pooled * pooled, axis=-1, keepdims=True) + EPSILON)
    ).astype(jnp.bfloat16)
    lane_vec = from_last_chip(lane_vec, chip)
    lane_vec, item_vec, slope = lax.optimization_barrier((lane_vec, item_vec, slope))
    other_vec = to_other_core(lane_vec)
    query_vec = jnp.concatenate(
        [jnp.where(core == 0, lane_vec, other_vec), jnp.where(core == 0, other_vec, lane_vec)],
        axis=0,
    )

    row_query = jnp.arange(count_rows, dtype=jnp.int32) // cand_count
    mine = row_query[:, None] == jnp.arange(query_count, dtype=jnp.int32)[None, :]
    products = lax.dot_general(
        item_vec, query_vec, (((1,), (1,)), ((), ())), preferred_element_type=jnp.float32
    )
    factor = query_scale[None, :] / math.sqrt(model_width)
    scores = query_scale[None, :] * products / math.sqrt(model_width) + cand_bias.reshape(-1)[:, None]
    highest = jnp.max(jnp.where(mine, scores, -jnp.inf), axis=0)
    shifted = jnp.exp(jnp.where(mine, scores - highest[None, :], -jnp.inf))
    summed = jnp.sum(shifted, axis=0)
    is_target = (jnp.arange(count_rows) % cand_count == 0)[:, None] & mine & (segment_idx == 0)
    positive = jnp.sum(jnp.where(is_target, scores, 0.0), axis=0)
    top, total, positive = combined_over_segment(jnp.stack([highest, summed, positive]))
    lse = top + jnp.log(total)
    query_loss = lse - positive

    widened = jnp.broadcast_to(
        query_vec.astype(jnp.float32)[:, None, :], (query_count, cand_count, model_width)
    ).reshape(count_rows, model_width)
    sloped = (widened * slope).astype(jnp.bfloat16)
    unscaled = lax.dot_general(
        sloped, item_weight, (((1,), (1,)), ((), ())), preferred_element_type=jnp.float32
    )
    unscaled, lse = lax.optimization_barrier((unscaled, lse))
    score_grad = jnp.exp(jnp.where(mine, scores - lse[None, :], -jnp.inf)) - is_target
    row_factor = jnp.sum(score_grad * factor, axis=1)
    row_grad = (unscaled * row_factor[:, None]).astype(jnp.bfloat16)
    grad_box = lax.dot_general(
        placed, row_grad, (((0,), (0,)), ((), ())), preferred_element_type=jnp.float32
    ).astype(jnp.bfloat16)
    got_grad = lax.all_to_all(
        grad_box.reshape(shard_count, capacity, -1), DP, split_axis=0, concat_axis=0, tiled=True
    ).reshape(slots, -1)
    table_grad = summed_over_segment(got_grad, inbox - 1, item_rows, chip, core)
    return (query_loss, table_grad)


def solution(mesh):
    return jax.shard_map(
        shards,
        mesh=mesh,
        in_specs=(
            P(DP, None, None),
            P(SEGMENT, None, None),
            P(SEGMENT, None),
            P(DP, None),
            P(),
            P(DP),
            P(DP, SEGMENT),
            P(DP, SEGMENT),
            P(DP, SEGMENT),
        ),
        out_specs=(P(DP), P(DP, None)),
        check_vma=False,
    )
```
